32 devices in a mesh: seq: 16 (over z, x, core), ch: 2 (over y).
Axes of the slice: x: 2, y: 2, z: 4, core: 2. Of those that a mesh axis runs over, the one named last changes fastest.
Arguments:
- hidden: bfloat16 [2048, 2048], P('seq', 'ch'), may hold values from -400 to 400, as said below
- tokens: int32 [2048], replicated, may hold values from 0 to 3
- edit_bounds: int32 [8, 2], replicated, may hold values from 0 to 2047
- norm_gain: float32 [2048], replicated, may hold values from 0.1 to 1.9
- base_embed: float32 [4, 2048], replicated, may hold values from -6 to 6
- w_in: bfloat16 [2, 2048, 4096], P(None, None, 'ch'), may hold values from -0.125 to 0.125
- conv_w: float32 [4, 4096], P(None, 'ch'), may hold values from -3 to 3
- conv_b: float32 [4096], P('ch'), may hold values from -3 to 3
- proj_bc: bfloat16 [32, 4096], P(None, 'ch'), may hold values from -0.1875 to 0.1875
- decay_rate: float32 [16, 4096], P(None, 'ch'), may hold values from 1.953125e-05 to 0.11, as said below
- skip_gain: float32 [4096], P('ch'), may hold values from -4 to 4
- w_out: bfloat16 [4096, 2048], P('ch'), may hold values from -0.09375 to 0.09375
Outputs:
- mixed: bfloat16 [2048, 2048], P('seq', 'ch')
The draws below stay inside these ranges and needn't reach their ends.
Inputs may be any that keep to these rules, and one draw needn't show every extreme that they name: The hidden states have row and column scales that differ. `decay_rate`: each entry is a positive decay rate per position. `edit_bounds`: positions in the window; a span's start and end come in no fixed order and may coincide with others.
All inputs are finite; a program needn't handle non-finite values.
Results may differ from the reference program's by a relative error of at most 0.014.
Values may be sent and summed in bfloat16 or wider, within the bound.
No kernel may reach another device: no remote copies, remote signals or barrier semaphores. Data moves between devices by JAX's collectives and lax.ppermute only.
A program may use at most 128 MiB of HBM per device.

```python
import math
import jax
import jax.numpy as jnp
from jax import lax

D = 2048
E = 4096
N = 16
CONV = 4
SPANS = 8
L_DEV = 128
TOTAL = 2048


def draw_hidden(key, part):
    first_key, second_key, third_key = jax.random.split(key, 3)
    base_values = jax.random.truncated_normal(first_key, -4.0, 4.0, (TOTAL, D), jnp.float32)
    row_scale = jnp.exp(jax.random.uniform(second_key, (TOTAL, 1), jnp.float32, 0.0, math.log(10.0)))
    column_scale = jnp.exp(jax.random.uniform(third_key, (1, D), jnp.float32, 0.0, math.log(10.0)))
    return (base_values * row_scale * column_scale).astype(jnp.bfloat16)


def draw_decay_rate(key, part):
    first_key, second_key, third_key = jax.random.split(key, 3)
    slow_share = 0.5
    slow_pick = jax.random.uniform(first_key, (N, E), jnp.float32) < slow_share
    slow_rate = jnp.exp(jax.random.uniform(second_key, (N, E), jnp.float32, math.log(0.05 / TOTAL), math.log(1.0 / TOTAL)))
    fast_rate = jnp.exp(jax.random.uniform(third_key, (N, E), jnp.float32, math.log(1.0 / 50.0), math.log(0.1)))
    return jnp.where(slow_pick, slow_rate, fast_rate)


def plant(values, stream_key, low, high):
    longest = values.shape.index(max(values.shape))
    spots = []
    for shift in (0, 1):
        where = [jax.random.randint(jax.random.fold_in(stream_key, axis), (), 0, length) for axis, length in enumerate(values.shape)]
        where[longest] = (where[longest] + shift) % values.shape[longest]
        spots.append(tuple(where))
    return values.at[spots[0]].set(low).at[spots[1]].set(high)


def block_scale(rng, dims, shards, low, top_value):
    loudness, own = 1.0, jax.random.fold_in(rng, 6)
    for dim, shards_of in shards:
        heights = jnp.exp(jax.random.uniform(jax.random.fold_in(own, dim), (shards_of,), jnp.float32, low / len(shards), top_value / len(shards)))
        loudness = loudness * jnp.repeat(heights, dims[dim] // shards_of).reshape([-1 if axis == dim else 1 for axis in range(len(dims))])
    return loudness


def scatter_about(stream_key, extent, scale, bound, pieces=(), kind=jnp.bfloat16):
    result = jax.random.normal(stream_key, extent, jnp.float32) * scale
    if len(pieces) > 0:
        result = block_scale(stream_key, extent, pieces, -0.22, 0.18) * result
    return jnp.clip(result, min=-bound, max=bound).astype(kind)


def setup_inputs(seed: int = 0) -> dict:
    arg_keys = jax.random.split(jax.random.key(seed), 13)
    hidden = draw_hidden(jax.random.fold_in(arg_keys[12], 71), 0)
    tokens = plant(jax.random.randint(arg_keys[1], (TOTAL,), 0, 4), jax.random.fold_in(arg_keys[1], 1), 0, 3).astype(jnp.int32)
    edit_bounds = plant(jax.random.randint(arg_keys[2], (SPANS, 2), 0, TOTAL), jax.random.fold_in(arg_keys[2], 1), 0, TOTAL - 1).astype(jnp.int32)
    norm_gain = jnp.clip(1.0 + 0.18 * jax.random.normal(arg_keys[3], (D,), jnp.float32), 0.1, 1.9)
    base_embed = scatter_about(arg_keys[4], (4, D), 1.0, 6.0, (), jnp.float32)
    w_in = scatter_about(arg_keys[5], (2, D, E), D ** -0.5, 0.125, ((2, 2),))
    conv_w = scatter_about(arg_keys[6], (CONV, E), CONV ** -0.5, 3.0, ((1, 2),), jnp.float32)
    conv_b = scatter_about(arg_keys[7], (E,), 0.5, 3.0, ((0, 2),), jnp.float32)
    proj_bc = scatter_about(arg_keys[8], (2 * N, E), (E // 4) ** -0.5, 0.1875, ((1, 2),))
    decay_rate = draw_decay_rate(jax.random.fold_in(arg_keys[12], 71), 0)
    skip_gain = scatter_about(arg_keys[10], (E,), 1.0, 4.0, ((0, 2),), jnp.float32)
    w_out = scatter_about(arg_keys[11], (E, D), E ** -0.5, 0.09375, ((0, 2),))
    return dict(hidden=hidden, tokens=tokens, edit_bounds=edit_bounds, norm_gain=norm_gain, base_embed=base_embed, w_in=w_in, conv_w=conv_w, conv_b=conv_b, proj_bc=proj_bc, decay_rate=decay_rate, skip_gain=skip_gain, w_out=w_out)


epsilon = 1e-05

def link(before, follow):
    return (before[0] * follow[0], before[1] * follow[0] + follow[1])

def run_stream(row_block, keep_rate, w_in, conv_w, conv_b, proj_bc, decay_rate, skip_gain):
    x_part = jnp.dot(row_block, w_in[0], preferred_element_type=jnp.float32).astype(jnp.bfloat16)
    z_part = jnp.dot(row_block, w_in[1], preferred_element_type=jnp.float32).astype(jnp.bfloat16)
    inner_width = x_part.shape[1]
    padded = jnp.concatenate([jnp.zeros((CONV - 1, inner_width), jnp.bfloat16), x_part], axis=0)
    conv_sum = conv_b[None, :] + jnp.zeros((TOTAL, inner_width), jnp.float32)
    for tap_index in range(CONV):
        conv_sum = conv_sum + padded[tap_index:tap_index + TOTAL].astype(jnp.float32) * conv_w[tap_index][None, :]
    mixed_in = jax.nn.silu(conv_sum).astype(jnp.bfloat16)
    inputs_bc = jnp.dot(proj_bc, mixed_in.T, preferred_element_type=jnp.float32)
    decay_mult = jnp.exp(-decay_rate)
    drive_gain = jnp.sqrt(-jnp.expm1(-2.0 * decay_rate))
    blocks = TOTAL // L_DEV
    block_inputs = (keep_rate.reshape(blocks, L_DEV), inputs_bc[:N].reshape(N, blocks, L_DEV).transpose(1, 0, 2), inputs_bc[N:].reshape(N, blocks, L_DEV).transpose(1, 0, 2), mixed_in.reshape(blocks, L_DEV, inner_width))

    def block_step(carry_in, block):
        keep_block, state_in, state_out, x_block = block
        x_float = x_block.astype(jnp.float32)
        decay_rows = keep_block[:, None, None] * decay_mult[None]
        drive_terms = drive_gain[None] * state_in.T[:, :, None] * x_float[:, None, :]
        cum_decay, local_state = lax.associative_scan(link, (decay_rows, drive_terms), axis=0)
        full_state = local_state + cum_decay * carry_in[None]
        y_out = jnp.einsum('nl,lne->le', state_out, full_state) + skip_gain[None] * x_float
        return (full_state[-1], y_out)
    zero_state = jnp.zeros((N, inner_width), jnp.float32)
    final_state, block_outputs = lax.scan(block_step, zero_state, block_inputs)
    y_all = block_outputs.reshape(TOTAL, inner_width)
    return (y_all * jax.nn.silu(z_part.astype(jnp.float32))).astype(jnp.bfloat16)

def reference(hidden, tokens, edit_bounds, norm_gain, base_embed, w_in, conv_w, conv_b, proj_bc, decay_rate, skip_gain, w_out):
    row_values = hidden.astype(jnp.float32)
    inv_rms = lax.rsqrt(lax.optimization_barrier(jnp.mean(row_values * row_values, axis=1, keepdims=True)) + epsilon)
    one_hot = (tokens[:, None] == jnp.arange(4, dtype=jnp.int32)[None, :]).astype(jnp.float32)
    embedded = one_hot[:, 0:1] * base_embed[0][None, :]
    for base_index in range(1, 4):
        embedded = embedded + one_hot[:, base_index:base_index + 1] * base_embed[base_index][None, :]
    normed = (row_values * inv_rms * norm_gain[None, :] + embedded).astype(jnp.bfloat16)
    places = jnp.arange(TOTAL, dtype=jnp.int32)
    hit_count = lax.optimization_barrier(jnp.sum((places[:, None] == edit_bounds.reshape(-1)[None, :]).astype(jnp.float32), axis=1))
    keep_rate = 1.0 / (1.0 + hit_count)
    forward_out = run_stream(normed, keep_rate, w_in, conv_w, conv_b, proj_bc, decay_rate, skip_gain)
    backward_out = run_stream(normed[::-1, ::-1], keep_rate[::-1], w_in, conv_w, conv_b, proj_bc, decay_rate, skip_gain)[::-1]
    summed = jnp.dot(forward_out, w_out, preferred_element_type=jnp.float32) + jnp.dot(backward_out, w_out, preferred_element_type=jnp.float32)[:, ::-1]
    return summed.astype(jnp.bfloat16)
```

```python
import functools

import jax
import jax.numpy as jnp
from jax import lax
from jax.experimental import pallas as pl
from jax.experimental.pallas import tpu as pltpu
from jax.sharding import PartitionSpec as P

CONV = 4
STATE = 16
EDGE = 16
LANES = 128
SUBS = 8
STREAMS = 2
VMEM_BYTES = 52 << 20
epsilon = 1e-05
f32 = jnp.float32
bf16 = jnp.bfloat16

WHOLE = pl.BlockSpec(memory_space=pltpu.VMEM)
SCALARS = pl.BlockSpec(memory_space=pltpu.SMEM)


def params():
    return pltpu.CompilerParams(vmem_limit_bytes=VMEM_BYTES)


def shaped(shape, dtype=f32):
    return jax.ShapeDtypeStruct(shape, dtype)


def swap(block, axis, apart):
    count = lax.axis_size(axis)
    return lax.ppermute(block, axis, [(i, i ^ apart) for i in range(count)])


def both_halves(block):
    if lax.axis_size("ch") == 2:
        return block, swap(block, "ch", 1), lax.axis_index("ch")
    full = lax.all_gather(block, "ch", axis=1, tiled=True)
    half = full.shape[1] // 2
    return full[:, :half], full[:, half:], jnp.int32(0)


def norm_kernel(flags, low, high, low_edge, high_edge, hot, gain, embed, out):
    rows = low.shape[0]
    half = low.shape[1]

    def one(first, second, first_row, count, scale):
        a = first[...].astype(f32)
        b = second[...].astype(f32)
        total = jnp.sum(a * a, axis=1, keepdims=True) + jnp.sum(b * b, axis=1, keepdims=True)
        inv_rms = lax.rsqrt(total / (2 * half) + epsilon)
        for part, values in enumerate((a, b)):
            cols = slice(part * half, (part + 1) * half)
            marks = hot[first_row : first_row + count, :]
            embedded = marks[:, 0:1] * embed[0:1, cols]
            for base in range(1, 4):
                embedded = embedded + marks[:, base : base + 1] * embed[base : base + 1, cols]
            normed = values * inv_rms * gain[0:1, cols] + embedded
            if scale is not None:
                normed = normed * scale
            out[first_row : first_row + count, cols] = normed.astype(bf16)

    valid = flags[1].astype(f32)

    @pl.when(flags[0] == 0)
    def _():
        one(low, high, 0, rows, None)
        one(low_edge, high_edge, rows, EDGE, valid)

    @pl.when(flags[0] != 0)
    def _():
        one(high, low, 0, rows, None)
        one(high_edge, low_edge, rows, EDGE, valid)


def signal_kernel(
    flags, own, other, w, conv_w, conv_b, proj, rows_out, c_out, bc_out, x_tiles, proj_rows, acc
):
    step = pl.program_id(0)
    rows = own.shape[0] - EDGE
    length = 2 * rows
    width = own.shape[1]
    padded = length + EDGE
    block = w.shape[2]
    tiles = block // LANES

    @pl.when(step == 0)
    def _():
        def place(first, second):
            rows_out[0:EDGE, :] = first[rows:, :]
            rows_out[EDGE : EDGE + rows, :] = first[:rows, :]
            rows_out[EDGE + rows : padded, :] = second[:rows, :]
            r = lax.broadcasted_iota(jnp.int32, (LANES, LANES), 0)
            q = lax.broadcasted_iota(jnp.int32, (LANES, LANES), 1)
            turn = jnp.where(r + q == LANES - 1, 1.0, 0.0).astype(bf16)
            for t in range(width // LANES):
                to = slice(t * LANES, (t + 1) * LANES)
                at = slice(width - (t + 1) * LANES, width - t * LANES)
                for base, piece in (
                    (0, first[:rows, at]),
                    (rows, second[:, at]),
                ):
                    turned = jnp.dot(piece, turn, preferred_element_type=f32)
                    rows_out[padded + base : padded + base + piece.shape[0], to] = turned.astype(
                        bf16
                    )

        @pl.when(flags[0] == 0)
        def _():
            place(own, other)

        @pl.when(flags[0] != 0)
        def _():
            place(other, own)

        proj_rows[...] = jnp.zeros(proj_rows.shape, bf16)
        acc[...] = jnp.zeros(acc.shape, f32)
        c_out[...] = jnp.zeros(c_out.shape, f32)

    x = jnp.dot(rows_out[...], w[0], preferred_element_type=f32).astype(bf16).astype(f32)
    for t in range(tiles):
        x_tiles[t] = x[:, t * LANES : (t + 1) * LANES]
    inner = 2 * STATE
    for s in range(STREAMS):
        mixed = []
        for t in range(tiles):
            cols = slice(t * LANES, (t + 1) * LANES)
            total = conv_b[0:1, cols]
            for k in range(CONV):
                at = EDGE - CONV + 1 + k if s == 0 else padded + CONV - 1 - k
                total = total + x_tiles[t, at : at + length, :] * conv_w[k : k + 1, cols]
            c = jax.nn.silu(total).astype(bf16)
            c_out[s, pl.ds(step * tiles + t, length, stride=SUBS), :] = c.astype(f32)
            mixed.append(c)
        mixed = mixed[0] if tiles == 1 else jnp.concatenate(mixed, axis=1)
        for half in range(2):
            i = 2 * half + s
            proj_rows[i, inner * i : inner * (i + 1), :] = proj[...]
            acc[...] += lax.dot_general(
                mixed[half * rows : (half + 1) * rows],
                proj_rows[i],
                (((1,), (1,)), ((), ())),
                preferred_element_type=f32,
            )

    @pl.when(step == pl.num_programs(0) - 1)
    def _():
        bc_out[...] = acc[...]


def gate_kernel(flags, rows_in, w, z_out):
    padded = rows_in.shape[0] // 2
    length = padded - EDGE
    z_out[0] = jnp.dot(rows_in[EDGE:padded, :], w[0], preferred_element_type=f32).astype(bf16)
    z_out[1] = jnp.dot(
        rows_in[padded : padded + length, :], w[0], preferred_element_type=f32
    ).astype(bf16)


def spread(bc, wide, slot, stream, first, rows):
    for n in range(STATE):
        for half in range(2):
            lane = 2 * STATE * (2 * half + stream) + first + n
            wide[slot + n, half * rows : (half + 1) * rows, :] = jnp.broadcast_to(
                bc[:, lane : lane + 1], (rows, LANES)
            )


def tile_at(ref, n):
    return ref[n * SUBS : (n + 1) * SUBS, :]


def end_kernel(bc_own, bc_far, weigh, c, decay, end_gain, bc_out, end_out, wide):
    rows = bc_own.shape[0]
    length = 2 * rows
    bc_out[...] = (bc_own[...] + bc_far[...]) * weigh[...]
    bc = bc_out[...]
    for s in range(STREAMS):
        spread(bc, wide, s * STATE, s, 0, rows)
    a = [tile_at(decay, n) for n in range(STATE)]

    def one(j, state):
        after = []
        for s in range(STREAMS):
            t = j if s == 0 else length - 1 - j
            x = c[s, pl.ds(pl.multiple_of(t * SUBS, SUBS), SUBS), :]
            for n in range(STATE):
                b = wide[s * STATE + n, pl.ds(t, 1), :]
                after.append(a[n] * state[s * STATE + n] + b * x)
        return tuple(after)

    zero = jnp.zeros((SUBS, LANES), f32)
    state = lax.fori_loop(0, length, one, (zero,) * (STREAMS * STATE), unroll=8)
    for s in range(STREAMS):
        for n in range(STATE):
            end_out[s, n * SUBS : (n + 1) * SUBS, :] = state[s * STATE + n] * tile_at(end_gain, n)


def local_kernel(stream, bc_in, c, decay, gain, skip, y_out, wide):
    rows = bc_in.shape[0]
    length = 2 * rows
    bc = bc_in[...]
    spread(bc, wide, 0, stream, 0, rows)
    spread(bc, wide, STATE, stream, STATE, rows)
    a = [tile_at(decay, n) for n in range(STATE)]
    g = [tile_at(gain, n) for n in range(STATE)]
    direct = skip[...]

    def one(j, state):
        t = j if stream == 0 else length - 1 - j
        at = pl.ds(pl.multiple_of(t * SUBS, SUBS), SUBS)
        x = c[0, at, :]
        after = []
        sums = [direct * x, None]
        for n in range(STATE):
            h = a[n] * state[n] + wide[n, pl.ds(t, 1), :] * (g[n] * x)
            after.append(h)
            term = wide[STATE + n, pl.ds(t, 1), :] * h
            sums[n % 2] = term if sums[n % 2] is None else sums[n % 2] + term
        y_out[at, :] = sums[0] + sums[1]
        return tuple(after)

    zero = jnp.zeros((SUBS, LANES), f32)
    lax.fori_loop(0, length, one, (zero,) * STATE, unroll=8)


def finish_kernel(
    flags, bc_in, entering, decay, y_f, y_b, z, w_hbm, send, keep, w, sem, wide, y, gated
):
    rows = bc_in.shape[0]
    length = 2 * rows
    inner = z.shape[2]
    width = w.shape[1]
    fetch = pltpu.make_async_copy(
        w_hbm.at[pl.ds(pl.multiple_of(flags[0] * inner, inner), inner), :], w, sem
    )
    fetch.start()
    bc = bc_in[...]
    for s in range(STREAMS):
        spread(bc, wide, s * STATE, s, STATE, rows)
    a = [tile_at(decay, n) for n in range(STATE)]
    before = (y_f, y_b)

    def one(j, state):
        after = []
        for s in range(STREAMS):
            t = j if s == 0 else length - 1 - j
            at = pl.ds(pl.multiple_of(t * SUBS, SUBS), SUBS)
            sums = [before[s][at, :], None]
            for n in range(STATE):
                h = a[n] * state[s * STATE + n]
                after.append(h)
                term = wide[s * STATE + n, pl.ds(t, 1), :] * h
                sums[n % 2] = term if sums[n % 2] is None else sums[n % 2] + term
            y[s, at, :] = sums[0] + sums[1]
        return tuple(after)

    start = tuple(
        entering[s, n * SUBS : (n + 1) * SUBS, :] for s in range(STREAMS) for n in range(STATE)
    )
    lax.fori_loop(0, length, one, start, unroll=4)
    for s in range(STREAMS):
        for t in range(inner // LANES):
            cols = slice(t * LANES, (t + 1) * LANES)
            values = y[s, pl.ds(t, length, stride=SUBS), :]
            gated[s, :, cols] = (values * jax.nn.silu(z[s, :, cols].astype(f32))).astype(bf16)
    fetch.wait()
    back = LANES - 1 - lax.broadcasted_iota(jnp.int32, (rows, LANES), 1)
    strip = min(2 * LANES, width)

    def put(near, half):
        where = slice(half * rows, (half + 1) * rows)
        for first in range(0, width, strip):
            ahead = jnp.dot(
                gated[0, where, :], w[:, first : first + strip], preferred_element_type=f32
            )
            behind = jnp.dot(
                gated[1, where, :],
                w[:, width - first - strip : width - first],
                preferred_element_type=f32,
            )
            for t in range(strip // LANES):
                mirrored = behind[:, strip - (t + 1) * LANES : strip - t * LANES]
                total = ahead[:, t * LANES : (t + 1) * LANES] + jnp.take_along_axis(
                    mirrored, back, axis=1
                )
                near[:, first + t * LANES : first + (t + 1) * LANES] = total.astype(near.dtype)

    @pl.when(flags[0] == 0)
    def _():
        put(send, 1)
        put(keep, 0)

    @pl.when(flags[0] != 0)
    def _():
        put(send, 0)
        put(keep, 1)


def as_tiles(values, tiles):
    spaced = values.reshape(values.shape[0], tiles, LANES)
    if tiles < SUBS:
        spaced = jnp.pad(spaced, ((0, 0), (0, SUBS - tiles), (0, 0)))
    return spaced.reshape(values.shape[0] * SUBS, LANES)


def body(
    hidden,
    tokens,
    edit_bounds,
    norm_gain,
    base_embed,
    w_in,
    conv_w,
    conv_b,
    proj_bc,
    decay_rate,
    skip_gain,
    w_out,
):
    rows = hidden.shape[0]
    width = w_in.shape[1]
    local = w_in.shape[2]
    inner = local // 2
    tiles = inner // LANES
    length = 2 * rows
    padded = length + EDGE
    seq_count = lax.axis_size("seq")
    ch_count = lax.axis_size("ch")
    chips = seq_count // 2
    place = lax.axis_index("seq")
    core = place % 2
    chip = place // 2

    first, second, exchanged = both_halves(hidden)
    rim = lax.dynamic_slice_in_dim(hidden, core * (rows - EDGE), EDGE)
    pairs = [(i, i + 1) for i in range(1, seq_count - 1, 2)]
    rim = lax.ppermute(rim, "seq", pairs + [(j, i) for i, j in pairs])
    rim_first, rim_second, _ = both_halves(rim)
    own_bases = lax.dynamic_slice_in_dim(tokens, place * rows, rows)
    rim_at = jnp.where(core == 0, place * rows - EDGE, (place + 1) * rows)
    rim_bases = lax.dynamic_slice_in_dim(
        tokens, jnp.clip(rim_at, 0, seq_count * rows - EDGE), EDGE
    )
    bases = jnp.concatenate([own_bases, rim_bases])
    hot = (bases[:, None] == jnp.arange(4, dtype=jnp.int32)[None, :]).astype(f32)
    valid = jnp.where(core == 0, place > 0, place < seq_count - 1)
    normed = pl.pallas_call(
        norm_kernel,
        out_shape=shaped((rows + EDGE, width), bf16),
        in_specs=[SCALARS] + [WHOLE] * 7,
        out_specs=WHOLE,
        compiler_params=params(),
        name="norm",
    )(
        jnp.stack([exchanged, valid.astype(jnp.int32)]),
        first,
        second,
        rim_first,
        rim_second,
        hot,
        norm_gain[None, :],
        base_embed,
    )
    partner = swap(normed, "seq", 1)

    marks = edit_bounds.reshape(-1)
    places = jnp.arange(seq_count * rows, dtype=jnp.int32)
    weight = 1.0 + jnp.sum((places[:, None] == marks[None, :]).astype(f32), axis=1)
    chip_weight = jnp.prod(weight.reshape(chips, length), axis=1)
    own_weight = lax.dynamic_slice_in_dim(weight, chip * length, length)
    before = places[:length, None] >= places[None, :length]
    run_f = jnp.prod(jnp.where(before, own_weight[None, :], 1.0), axis=1)
    run_b = jnp.prod(jnp.where(before.T, own_weight[None, :], 1.0), axis=1)
    runs = jnp.stack([run_f, run_b]).reshape(2, 2, rows)
    pairs_bc = jnp.stack([runs, 1.0 / runs], axis=2)
    weigh = jnp.broadcast_to(
        pairs_bc.transpose(3, 1, 0, 2)[..., None], (rows, 2, STREAMS, 2, STATE)
    ).reshape(rows, 4 * 2 * STATE)

    rate = as_tiles(lax.dynamic_slice_in_dim(decay_rate, core * inner, inner, 1), tiles)
    decay = jnp.exp(-rate)
    gain = jnp.sqrt(-jnp.expm1(-2.0 * rate))
    skip = as_tiles(lax.dynamic_slice_in_dim(skip_gain, core * inner, inner)[None, :], tiles)
    own_keep = 1.0 / jnp.prod(own_weight)

    block = min(2 * LANES, inner)
    steps = inner // block
    whole = lambda shape: pl.BlockSpec(shape, lambda i, f: (0,) * len(shape))
    flags = core[None]
    stacked, c, bc = pl.pallas_call(
        signal_kernel,
        grid_spec=pltpu.PrefetchScalarGridSpec(
            num_scalar_prefetch=1,
            grid=(steps,),
            in_specs=[
                whole((rows + EDGE, width)),
                whole((rows + EDGE, width)),
                pl.BlockSpec((1, width, block), lambda i, f: (0, 0, f[0] * steps + i)),
                pl.BlockSpec((CONV, block), lambda i, f: (0, f[0] * steps + i)),
                pl.BlockSpec((1, block), lambda i, f: (0, f[0] * steps + i)),
                pl.BlockSpec((2 * STATE, block), lambda i, f: (0, f[0] * steps + i)),
            ],
            out_specs=[
                whole((2 * padded, width)),
                whole((STREAMS, length * SUBS, LANES)),
                whole((rows, LANES)),
            ],
            scratch_shapes=[
                pltpu.VMEM((block // LANES, 2 * padded, LANES), f32),
                pltpu.VMEM((4, LANES, block), bf16),
                pltpu.VMEM((rows, LANES), f32),
            ],
        ),
        out_shape=[
            shaped((2 * padded, width), bf16),
            shaped((STREAMS, length * SUBS, LANES)),
            shaped((rows, LANES)),
        ],
        compiler_params=params(),
        name="signal",
    )(flags, normed, partner, w_in, conv_w, conv_b[None, :], proj_bc)

    bc = bc + swap(bc, "seq", 1)
    if ch_count == 2:
        bc_far = swap(bc, "ch", 1)
    else:
        bc, bc_far = lax.psum(bc, "ch"), jnp.zeros_like(bc)

    z = pl.pallas_call(
        gate_kernel,
        grid_spec=pltpu.PrefetchScalarGridSpec(
            num_scalar_prefetch=1,
            grid=(steps,),
            in_specs=[
                whole((2 * padded, width)),
                pl.BlockSpec((1, width, block), lambda i, f: (1, 0, f[0] * steps + i)),
            ],
            out_specs=pl.BlockSpec((STREAMS, length, block), lambda i, f: (0, 0, i)),
        ),
        out_shape=shaped((STREAMS, length, inner), bf16),
        compiler_params=params(),
        name="gate",
    )(flags, stacked, w_in)

    scaled, ends = pl.pallas_call(
        end_kernel,
        out_shape=[shaped((rows, LANES)), shaped((STREAMS, STATE * SUBS, LANES))],
        in_specs=[WHOLE] * 6,
        out_specs=[WHOLE] * 2,
        scratch_shapes=[pltpu.VMEM((STREAMS * STATE, length, LANES), f32)],
        compiler_params=params(),
        name="ends",
    )(bc, bc_far, weigh, c, decay, gain * own_keep)

    local_y = []
    for s in range(STREAMS):
        local_y.append(
            pl.pallas_call(
                functools.partial(local_kernel, s),
                grid=(1,),
                out_shape=shaped((length * SUBS, LANES)),
                in_specs=[
                    pl.BlockSpec((rows, LANES), lambda i: (0, 0)),
                    pl.BlockSpec((1, length * SUBS, LANES), lambda i, s=s: (s, 0, 0)),
                    pl.BlockSpec((STATE * SUBS, LANES), lambda i: (0, 0)),
                    pl.BlockSpec((STATE * SUBS, LANES), lambda i: (0, 0)),
                    pl.BlockSpec((SUBS, LANES), lambda i: (0, 0)),
                ],
                out_specs=pl.BlockSpec((length * SUBS, LANES), lambda i: (0, 0)),
                scratch_shapes=[pltpu.VMEM((2 * STATE, length, LANES), f32)],
                compiler_params=params(),
                name="local",
            )(scaled, c, decay, gain, skip)
        )

    spots = jnp.arange(chips, dtype=jnp.int32)
    keep_of = lambda mask: 1.0 / jnp.prod(jnp.where(mask, chip_weight, 1.0))
    group = ends
    entering = jnp.zeros_like(ends)
    levels = chips.bit_length() - 1
    for level in range(levels):
        size = 1 << level
        upper = (chip >> level) & 1 == 1
        mine = spots >> level == chip >> level
        theirs = spots >> level == (chip >> level) ^ 1
        inside = chip & (size - 1)
        span = jnp.exp(rate * (-float(length * size)))
        ahead = jnp.exp(rate * (-float(length) * inside.astype(f32)))
        behind = jnp.exp(rate * (-float(length) * (size - 1 - inside).astype(f32)))
        ahead = ahead * keep_of(mine & (spots < chip))
        behind = behind * keep_of(mine & (spots > chip))
        if level == levels - 1:
            got = swap(jnp.where(upper, group[1], group[0]).astype(bf16), "seq", 2 * size)
            got = jnp.stack([got, got]).astype(f32)
        else:
            got = swap(group.astype(bf16), "seq", 2 * size).astype(f32)
        follows = jnp.stack([upper, ~upper])[:, None, None]
        lead = jnp.stack([ahead, behind])
        entering = entering + jnp.where(follows, lead * got, 0.0)
        if level < levels - 1:
            group = jnp.where(
                follows,
                got * (span * keep_of(mine))[None] + group,
                group * (span * keep_of(theirs))[None] + got,
            )

    send, keep = pl.pallas_call(
        finish_kernel,
        out_shape=[shaped((rows, width), bf16), shaped((rows, width))],
        in_specs=[SCALARS] + [WHOLE] * 6 + [pl.BlockSpec(memory_space=pl.ANY)],
        out_specs=[WHOLE] * 2,
        scratch_shapes=[
            pltpu.VMEM((inner, width), bf16),
            pltpu.SemaphoreType.DMA,
            pltpu.VMEM((STREAMS * STATE, length, LANES), f32),
            pltpu.VMEM((STREAMS, length * SUBS, LANES), f32),
            pltpu.VMEM((STREAMS, length, inner), bf16),
        ],
        compiler_params=params(),
        name="finish",
    )(flags, scaled, entering, decay, local_y[0], local_y[1], z, w_out)
    total = keep + swap(send, "seq", 1).astype(f32)
    if ch_count != 2:
        return lax.psum_scatter(total.astype(bf16), "ch", scatter_dimension=1, tiled=True)
    half = width // 2
    where = lax.axis_index("ch")
    theirs = lax.dynamic_slice_in_dim(total, (1 - where) * half, half, 1).astype(bf16)
    mine = lax.dynamic_slice_in_dim(total, where * half, half, 1)
    return (mine + swap(theirs, "ch", 1).astype(f32)).astype(bf16)


def solution(mesh):
    placed = (
        P("seq", "ch"),
        P(),
        P(),
        P(),
        P(),
        P(None, None, "ch"),
        P(None, "ch"),
        P("ch"),
        P(None, "ch"),
        P(None, "ch"),
        P("ch"),
        P("ch", None),
    )
    return jax.shard_map(
        body, mesh=mesh, in_specs=placed, out_specs=P("seq", "ch"), check_vma=False
    )
```

```python
import functools

import jax
import jax.numpy as jnp
from jax import lax
from jax.experimental import pallas as pl
from jax.experimental.pallas import tpu as pltpu
from jax.sharding import PartitionSpec as P

CONV = 4
STATE = 16
EDGE = 16
LANES = 128
SUBS = 8
STREAMS = 2
CHUNK = 16
BLOCK = 256
HALVES = 2
epsilon = 1e-05
f32 = jnp.float32
bf16 = jnp.bfloat16

WHOLE = pl.BlockSpec(memory_space=pltpu.VMEM)
SCALARS = pl.BlockSpec(memory_space=pltpu.SMEM)
ANYWHERE = pl.BlockSpec(memory_space=pltpu.HBM)


def shaped(shape, dtype=f32):
    return jax.ShapeDtypeStruct(shape, dtype)


def call(kernel, name, outs, ins, scratch=(), megabytes=4):
    return pl.pallas_call(
        kernel,
        out_shape=outs,
        in_specs=ins,
        out_specs=jax.tree.map(lambda _: WHOLE, outs),
        scratch_shapes=list(scratch),
        compiler_params=pltpu.CompilerParams(vmem_limit_bytes=megabytes << 20),
        name=name,
    )


def tile(t):
    return slice(t * LANES, (t + 1) * LANES)


def spot():
    place = lax.axis_index("seq")
    return place, place & 1, place >> 1


def swap(block, axis, apart):
    count = lax.axis_size(axis)
    return lax.ppermute(block, axis, [(i, i ^ apart) for i in range(count)])


def in_hbm(array):
    return pltpu.with_memory_space_constraint(array, pltpu.HBM)


def both_halves(block):
    if lax.axis_size("ch") == 2:
        return block, swap(block, "ch", 1)
    full = lax.all_gather(block, "ch", axis=1, tiled=True)
    half = full.shape[1] // 2
    return full[:, :half], full[:, half:]


def rims(rim):
    seq_count, ch_count = lax.axis_size("seq"), lax.axis_size("ch")
    pairs = [(i, i + 1) for i in range(1, seq_count - 1, 2)]
    pairs = pairs + [(j, i) for i, j in pairs]
    if ch_count != 2:
        return both_halves(lax.ppermute(rim, "seq", pairs))
    return tuple(
        lax.ppermute(
            rim,
            ("seq", "ch"),
            [(i * ch_count + (k ^ apart), j * ch_count + k) for i, j in pairs for k in range(2)],
        )
        for apart in range(2)
    )


def between(chip, m):
    pair = chip >> 1
    other = pair ^ m
    below = other < pair
    return jnp.where(below, 2 * other + 2, chip + 1), jnp.where(below, chip, 2 * other), below


def init_kernel(
    bounds, tokens_all, w_in, conv_w, conv_b, proj, rate_all, skip, gain_all, embed_all, hidden,
    signal_w, taps, offset, proj_half, rate, skip_half, norm_gain, embed, rim,
    bases, weigh, decay, keeps, tokens, sems,
):
    place, core, chip = spot()
    count, rows = tokens.shape
    length = 2 * rows
    inner = signal_w.shape[1]
    chips = count // 2
    mine = pl.ds(pl.multiple_of(core * inner, inner), inner)
    copies = [
        pltpu.make_async_copy(source, target, sems.at[i])
        for i, (source, target) in enumerate(
            (
                (rate_all.at[:, mine], rate),
                (tokens_all, tokens),
                (gain_all, norm_gain),
                (embed_all, embed),
                (conv_w.at[:, mine], taps),
                (conv_b.at[:, mine], offset),
                (proj.at[:, mine], proj_half),
                (skip.at[:, mine], skip_half),
                (
                    hidden.at[pl.ds(pl.multiple_of(core * (rows - EDGE), EDGE), EDGE), :],
                    rim,
                ),
                (w_in.at[0, :, mine], signal_w),
            )
        )
    ]
    for copy in copies:
        copy.start()

    marks = [bounds[k, i] for i in range(bounds.shape[1]) for k in range(2)]
    factors = []
    for i, mark in enumerate(marks):
        total = jnp.int32(1)
        earlier = jnp.int32(0)
        for k, other in enumerate(marks):
            same = jnp.where(other == mark, 1, 0)
            total = total + same
            if k < i:
                earlier = earlier + same
        factors.append(jnp.where(earlier > 0, 1, total).astype(f32))

    start = chip * length
    at = lax.broadcasted_iota(jnp.int32, (SUBS, rows), 1) + start
    for half in range(HALVES):
        runs = [jnp.ones((SUBS, rows), f32) for _ in range(STREAMS)]
        for mark, factor in zip(marks, factors):
            here = at + half * rows
            runs[0] = runs[0] * jnp.where((here >= mark) & (mark >= start), factor, 1.0)
            runs[1] = runs[1] * jnp.where((here <= mark) & (mark < start + length), factor, 1.0)
        for s in range(STREAMS):
            first = 2 * STATE * (2 * half + s)
            for k in range(STATE // SUBS):
                weigh[first + k * SUBS : first + (k + 1) * SUBS, :] = runs[s]
                low = first + STATE + k * SUBS
                weigh[low : low + SUBS, :] = 1.0 / runs[s]

    def kept(low, high):
        total = jnp.ones((SUBS, LANES), f32)
        for mark, factor in zip(marks, factors):
            total = total * jnp.where(
                (mark >= low * length) & (mark < high * length), factor, 1.0
            )
        return 1.0 / total

    keeps[0] = kept(chip, chip + 1)
    keeps[1] = kept(chip ^ 1, (chip ^ 1) + 1)
    for m in range(1, chips // 2):
        low, high, _ = between(chip, m)
        keeps[1 + m] = kept(low, high)
    copies[0].wait()
    for t in range(inner // LANES):
        decay[:, tile(t)] = jnp.exp(-rate[:, tile(t)])

    copies[1].wait()

    def column(row):
        line = tokens[pl.ds(row, 1), :].astype(f32)
        return jnp.broadcast_to(line, (rows, rows)).T

    bases[:rows, :] = column(place)
    beyond = column(jnp.clip(jnp.where(core == 0, place - 1, place + 1), 0, count - 1))
    beyond = jnp.where(core == 0, beyond[rows - EDGE :], beyond[:EDGE])
    inside = jnp.where(core == 0, place > 0, place < count - 1)
    bases[rows:, :] = jnp.where(inside, beyond, -1.0)
    for copy in copies[2:]:
        copy.wait()


def norm_kernel(own, far, own_rim, far_rim, bases, gain, embed, out):
    rows = own.shape[0]
    half = own.shape[1]
    index = lax.axis_index("ch") if lax.axis_size("ch") == 2 else jnp.int32(0)

    def one(first, second, low, count):
        marks = bases[low : low + count, :]
        total = jnp.zeros((count, LANES), f32)
        for part in (first, second):
            for t in range(half // LANES):
                v = part[:, tile(t)].astype(f32)
                total = total + v * v
        inv_rms = lax.rsqrt(jnp.sum(total, axis=1, keepdims=True) / (2 * half) + epsilon)
        inv_rms = jnp.broadcast_to(inv_rms, (count, LANES))
        for k, part in enumerate((first, second)):
            for t in range(half // LANES):
                cols = slice(k * half + t * LANES, k * half + (t + 1) * LANES)
                e = [embed[b : b + 1, cols] for b in range(4)]
                added = jnp.where(
                    marks < 0.5, e[0], jnp.where(marks < 1.5, e[1], jnp.where(marks < 2.5, e[2], e[3]))
                )
                v = part[:, tile(t)].astype(f32) * inv_rms * gain[0:1, cols] + added
                out[low : low + count, cols] = jnp.where(marks < -0.5, 0.0, v).astype(bf16)

    @pl.when(index == 0)
    def _():
        one(own, far, 0, rows)
        one(own_rim, far_rim, rows, EDGE)

    @pl.when(index != 0)
    def _():
        one(far, own, 0, rows)
        one(far_rim, own_rim, rows, EDGE)


def signal_kernel(
    own, other, w, taps, offset, proj, w_in, lined, c_out, bc_out, gate_w, x_tiles, sem
):
    _, core, _ = spot()
    rows = own.shape[0] - EDGE
    length = 2 * rows
    width = own.shape[1]
    padded = length + EDGE
    inner = w.shape[1]
    block = min(BLOCK, inner)
    tiles = block // LANES
    fetch = pltpu.make_async_copy(
        w_in.at[1, :, pl.ds(pl.multiple_of(core * inner, inner), inner)], gate_w, sem
    )
    fetch.start()

    def line_up(first, second):
        lined[0:EDGE, :] = first[rows:, :]
        lined[EDGE : EDGE + rows, :] = first[:rows, :]
        lined[EDGE + rows : padded, :] = second[:rows, :]
        r = lax.broadcasted_iota(jnp.int32, (LANES, LANES), 0)
        q = lax.broadcasted_iota(jnp.int32, (LANES, LANES), 1)
        turn = jnp.where(r + q == LANES - 1, 1.0, 0.0).astype(bf16)
        for t in range(width // LANES):
            at = tile(width // LANES - 1 - t)
            for base, piece in ((0, first[:rows, at]), (rows, second[:, at])):
                turned = jnp.dot(piece, turn, preferred_element_type=f32).astype(bf16)
                lined[padded + base : padded + base + piece.shape[0], tile(t)] = turned

    @pl.when(core == 0)
    def _():
        line_up(own, other)

    @pl.when(core != 0)
    def _():
        line_up(other, own)

    inner_bc = 2 * STATE
    sums = [jnp.zeros((inner_bc, rows), f32) for _ in range(STREAMS * HALVES)]

    def project(b, s):
        x = jnp.dot(
            lined[s * padded : (s + 1) * padded, :],
            w[:, b * block : (b + 1) * block],
            preferred_element_type=f32,
        )
        x = x.astype(bf16).astype(f32)
        for t in range(tiles):
            x_tiles[(b % 2 * STREAMS + s) * tiles + t] = x[:, tile(t)]

    def convolve(b, s):
        mixed = []
        for t in range(tiles):
            slot = (b % 2 * STREAMS + s) * tiles + t
            cols = tile(b * tiles + t)
            total = offset[0:1, cols]
            for k in range(CONV):
                at = EDGE - CONV + 1 + k if s == 0 else CONV - 1 - k
                total = total + x_tiles[slot, at : at + length, :] * taps[k : k + 1, cols]
            c = jax.nn.silu(total).astype(bf16)
            c_out[s, b * tiles + t] = c.astype(f32)
            mixed.append(c)
        mixed = mixed[0] if tiles == 1 else jnp.concatenate(mixed, axis=1)
        for half in range(HALVES):
            sums[2 * half + s] = sums[2 * half + s] + lax.dot_general(
                proj[:, b * block : (b + 1) * block],
                mixed[half * rows : (half + 1) * rows],
                (((1,), (1,)), ((), ())),
                preferred_element_type=f32,
            )

    turns = [(b, s) for b in range(inner // block) for s in range(STREAMS)]
    project(*turns[0])
    for before, after in zip(turns, turns[1:] + [None]):
        if after is not None:
            project(*after)
        convolve(*before)
    for i, total in enumerate(sums):
        bc_out[i * inner_bc : (i + 1) * inner_bc, :] = total
    fetch.wait()


def gate_kernel(lined, w, z_out):
    padded = lined.shape[0] // 2
    length = padded - EDGE
    inner = w.shape[1]
    block = min(BLOCK, inner)
    for b in range(inner // block):
        cols = slice(b * block, (b + 1) * block)
        for s, first in ((0, EDGE), (1, padded)):
            z = jnp.dot(lined[first : first + length, :], w[:, cols], preferred_element_type=f32)
            z_out[s, :, cols] = z.astype(bf16)


def lane_of(values, lane):
    return jnp.take_along_axis(values, jnp.full(values.shape, lane, jnp.int32), axis=1)


def tiles_of(ref, count):
    return [ref[h * SUBS : (h + 1) * SUBS, tile(t)] for t in range(count) for h in range(2)]


def spread(bc, wide, stream):
    rows = bc.shape[1]
    ones = jnp.ones((2 * rows, LANES), bf16)
    lanes = lax.broadcasted_iota(jnp.int32, (STATE, 2 * rows), 1) & (rows - 1)
    group = 8
    for half in range(HALVES):
        first = 2 * STATE * (2 * half + stream)
        exact = bc[first : first + STATE, :]
        high = exact.astype(bf16)
        low = (exact - high.astype(f32)).astype(bf16)
        entries = jnp.concatenate([high, low], axis=1).astype(f32)
        for j in range(0, rows, group):
            alone = jnp.concatenate(
                [jnp.where(lanes == j + i, entries, 0.0).astype(bf16) for i in range(group)], axis=0
            )
            at = (half * rows + j) * STATE
            wide[stream, at : at + group * STATE, :] = jnp.dot(
                alone, ones, preferred_element_type=f32
            )


def end_kernel(bc_own, bc_far, weigh, c, decay, end_gain, after_z, bc_out, end_out, wide):
    rows = bc_own.shape[1]
    length = 2 * rows
    count = c.shape[1]
    bc_out[...] = (bc_own[...] + bc_far[...]) * weigh[...]
    for s in range(STREAMS):
        spread(bc_out, wide, s)
    a = tiles_of(decay, count)

    def one(j, state):
        after = []
        for s in range(STREAMS):
            t0 = j if s == 0 else length - 1 - j
            low = pl.multiple_of(t0 * STATE, STATE)
            b = [wide[s, pl.ds(low + h * SUBS, SUBS), :] for h in range(2)]
            for t in range(count):
                x = c[s, t, pl.ds(t0, 1), :]
                for h in range(2):
                    i = 2 * t + h
                    after.append(a[i] * state[s * 2 * count + i] + b[h] * x)
        return tuple(after)

    zero = jnp.zeros((SUBS, LANES), f32)
    state = lax.fori_loop(0, length, one, (zero,) * (STREAMS * 2 * count), unroll=8)
    for s in range(STREAMS):
        for t in range(count):
            for h in range(2):
                sub = slice(h * SUBS, (h + 1) * SUBS)
                end_out[s, sub, tile(t)] = state[s * 2 * count + 2 * t + h] * end_gain[sub, tile(t)]


def local_kernel(stream, bc, wide, c, decay, drive, skip, after_got, *rest):
    if stream == 1:
        w_out, y_out, readout, out_w, driven, sem = rest
        inner = decay.shape[1]
        mine = pl.ds(pl.multiple_of(spot()[1] * inner, inner), inner)
        fetch = pltpu.make_async_copy(w_out.at[mine, :], out_w, sem)
        fetch.start()
    else:
        y_out, readout, driven = rest
    rows = bc.shape[1]
    length = 2 * rows
    count = c.shape[1]
    span = CHUNK * STATE
    turned = bc[...].T.astype(bf16)
    for half in range(HALVES):
        r = lax.broadcasted_iota(jnp.int32, (rows, span), 0)
        q = lax.broadcasted_iota(jnp.int32, (rows, span), 1)
        first = 2 * STATE * (2 * half + stream) + STATE
        pick = jnp.where(r == first + (q & (STATE - 1)), 1.0, 0.0).astype(bf16)
        picked = jnp.dot(turned, pick, preferred_element_type=f32)
        step = r & (CHUNK - 1) if stream == 0 else CHUNK - 1 - (r & (CHUNK - 1))
        readout[half * rows : (half + 1) * rows, :] = jnp.where(
            q // STATE == step, picked, 0.0
        ).astype(bf16)
    a = tiles_of(decay, count)

    def chunks(n, state):
        state = list(state)
        base = n * CHUNK if stream == 0 else length - (n + 1) * CHUNK
        base = pl.multiple_of(base, CHUNK)
        low = pl.multiple_of(base * STATE, span)
        to = pl.multiple_of(n * span, span)
        for j in range(CHUNK):
            i = j if stream == 0 else CHUNK - 1 - j
            b = [wide[stream, pl.ds(low + i * STATE + h * SUBS, SUBS), :] for h in range(2)]
            for t in range(count):
                x = c[stream, t, pl.ds(base + i, 1), :]
                for h in range(2):
                    m = 2 * t + h
                    state[m] = a[m] * state[m] + b[h] * x
                both = jnp.concatenate([state[2 * t], state[2 * t + 1]], axis=0)
                driven[pl.ds(to + j * STATE, STATE), tile(t)] = (
                    both.astype(bf16) * drive[:, tile(t)]
                )
        return tuple(state)

    zero = jnp.zeros((SUBS, LANES), f32)
    lax.fori_loop(0, length // CHUNK, chunks, (zero,) * (2 * count))
    for n in range(length // CHUNK):
        base = n * CHUNK if stream == 0 else length - (n + 1) * CHUNK
        at = slice(base, base + CHUNK)
        y = jnp.dot(
            readout[at, :], driven[n * span : (n + 1) * span, :], preferred_element_type=f32
        )
        for t in range(count):
            y_out[at, tile(t)] = y[:, tile(t)] + skip[0:1, tile(t)] * c[stream, t, at, :]
    if stream == 1:
        fetch.wait()


def factor_kernel(rate, keeps, after_ends, strides, powers, first_step, leads):
    _, _, chip = spot()
    inner = rate.shape[1]
    upper = chip & 1
    for t in range(inner // LANES):
        d = rate[:, tile(t)]
        a = jnp.exp(-d)
        strides[0, :, tile(t)] = jnp.exp(-float(CHUNK) * d)
        strides[1, :, tile(t)] = jnp.exp(-float(LANES) * d)
        power = a
        for j in range(CHUNK):
            powers[j * STATE : (j + 1) * STATE, tile(t)] = power.astype(bf16)
            power = power * a
        d = d * float(-2 * LANES)
        span = jnp.exp(d)
        own = span * keeps[0, 0:1, :]
        beside = span * keeps[1, 0:1, :]
        first_step[0, 0, :, tile(t)] = jnp.where(upper == 1, own, 1.0)
        first_step[0, 1, :, tile(t)] = jnp.where(upper == 1, 1.0, own)
        first_step[1, 0, :, tile(t)] = jnp.where(upper == 1, 1.0, beside)
        first_step[1, 1, :, tile(t)] = jnp.where(upper == 1, beside, 1.0)
        for m in range(1, keeps.shape[0] - 1):
            low, high, below = between(chip, m)
            lead = jnp.exp(d * (high - low).astype(f32)) * keeps[1 + m, 0:1, :]
            leads[m - 1, 0, :, tile(t)] = jnp.where(below, lead, 0.0)
            leads[m - 1, 1, :, tile(t)] = jnp.where(below, 0.0, lead)


def pair_kernel(ends, got, first_step, after_local, *sends):
    _, _, chip = spot()
    group = [
        (got[s].astype(f32) * first_step[0, s] + ends[s] * first_step[1, s]).astype(bf16)
        for s in range(STREAMS)
    ]
    for m, send in enumerate(sends):
        _, _, below = between(chip, m + 1)
        send[...] = jnp.where(below, group[1], group[0])


def columns(gated, w, out, part):
    inner, width = w.shape
    rows, half = out.shape
    base = pl.multiple_of(part * half, half)
    back = LANES - 1 - lax.broadcasted_iota(jnp.int32, (rows, LANES), 1)
    strip = min(BLOCK, half)
    for low in range(0, half, strip):
        here = pl.ds(pl.multiple_of(base + low, strip), strip)
        there = pl.ds(pl.multiple_of(width - base - low - strip, strip), strip)
        ahead = jnp.dot(gated[0], w[:, here], preferred_element_type=f32)
        behind = jnp.dot(gated[1], w[:, there], preferred_element_type=f32)
        for t in range(strip // LANES):
            turned = jnp.take_along_axis(behind[:, tile(strip // LANES - 1 - t)], back, axis=1)
            total = ahead[:, tile(t)] + turned
            out[:, low + t * LANES : low + (t + 1) * LANES] = total.astype(out.dtype)


def part_of(own):
    if lax.axis_size("ch") != 2:
        return jnp.int32(1 if own else 0)
    return lax.axis_index("ch") if own else 1 - lax.axis_index("ch")


def finish_kernel(
    same, powers, strides, got, leads, y_f, y_b, readout_f, readout_b, z, w, *rest
):
    *arrived, out, gated = rest
    _, core, chip = spot()
    rows = out.shape[0]
    inner = w.shape[0]
    half = core if same else 1 - core
    base = pl.multiple_of(half * rows, rows)
    span = CHUNK * STATE
    local = (y_f, y_b)
    readouts = (readout_f, readout_b)
    for s in range(STREAMS):
        state = got[s].astype(f32) * jnp.where(chip & 1 == 1 - s, 1.0, 0.0)
        for m, part in enumerate(arrived):
            state = state + part[...].astype(f32) * leads[m, s]
        state = state * jnp.where(half == 1 - s, strides[1], 1.0)
        for q in range(rows // CHUNK):
            row = q * CHUNK if s == 0 else rows - (q + 1) * CHUNK
            at = pl.ds(pl.multiple_of(base + row, CHUNK), CHUNK)
            carried = powers[...].reshape(CHUNK, STATE, inner) * state.astype(bf16)[None]
            state = state * strides[0]
            y = jnp.dot(
                readouts[s][at, :], carried.reshape(span, inner), preferred_element_type=f32
            )
            y = y + local[s][at, :]
            gated[s, row : row + CHUNK, :] = (
                y * jax.nn.silu(z[s, at, :].astype(f32))
            ).astype(bf16)
    columns(gated, w, out, part_of(False))


def rest_kernel(gated, w, after_first, out):
    columns(gated, w, out, part_of(True))


def body(
    hidden,
    tokens,
    edit_bounds,
    norm_gain,
    base_embed,
    w_in,
    conv_w,
    conv_b,
    proj_bc,
    decay_rate,
    skip_gain,
    w_out,
):
    rows = hidden.shape[0]
    width = w_in.shape[1]
    inner = w_in.shape[2] // 2
    tiles = inner // LANES
    length = 2 * rows
    padded = length + EDGE
    block = min(BLOCK, inner)
    seq_count = lax.axis_size("seq")
    ch_count = lax.axis_size("ch")
    chips = seq_count // 2
    chip = spot()[2]

    first, second = both_halves(hidden)
    channels = (STATE, inner)
    pairs = chips // 2
    (
        signal_w, taps, offset, proj_half, rate, skip, gain, embed, rim,
        bases, weigh, decay, keeps,
    ) = call(
        init_kernel,
        "init",
        [
            shaped((width, inner), bf16),
            shaped((CONV, inner)),
            shaped((1, inner)),
            shaped((2 * STATE, inner), bf16),
            shaped(channels),
            shaped((1, inner)),
            shaped((1, width)),
            shaped((4, width)),
            shaped((EDGE, hidden.shape[1]), bf16),
            shaped((rows + EDGE, LANES)),
            shaped((4 * 2 * STATE, rows)),
            shaped(channels),
            shaped((max(pairs, 1) + 1, SUBS, LANES)),
        ],
        [SCALARS] + [ANYWHERE] * 10,
        [pltpu.VMEM((seq_count, rows), jnp.int32), pltpu.SemaphoreType.DMA((10,))],
    )(
        edit_bounds.T,
        *(
            in_hbm(array)
            for array in (
                tokens.reshape(seq_count, rows),
                w_in,
                conv_w,
                conv_b[None, :],
                proj_bc,
                decay_rate,
                skip_gain[None, :],
                norm_gain[None, :],
                base_embed,
                hidden,
            )
        ),
    )
    rim_first, rim_second = rims(rim)
    drive = jnp.sqrt(-jnp.expm1(-2.0 * rate))
    normed = call(norm_kernel, "norm", shaped((rows + EDGE, width), bf16), [WHOLE] * 7)(
        first, second, rim_first, rim_second, bases, gain, embed
    )
    partner = swap(normed, "seq", 1)

    lined, c, bc, gate_w = call(
        signal_kernel,
        "signal",
        [
            shaped((2 * padded, width), bf16),
            shaped((STREAMS, tiles, length, LANES)),
            shaped((4 * 2 * STATE, rows)),
            shaped((width, inner), bf16),
        ],
        [WHOLE] * 6 + [ANYWHERE],
        [
            pltpu.VMEM((2 * STREAMS * block // LANES, padded, LANES), f32),
            pltpu.SemaphoreType.DMA,
        ],
        megabytes=6,
    )(normed, partner, signal_w, taps, offset, proj_half, in_hbm(w_in))
    bc = bc + swap(bc, "seq", 1)
    if ch_count == 2:
        bc_far = swap(bc, "ch", 1)
    else:
        bc, bc_far = lax.psum(bc, "ch"), jnp.zeros_like(bc)

    z = call(gate_kernel, "gate", shaped((STREAMS, length, inner), bf16), [WHOLE] * 2)(
        lined, gate_w
    )
    later = pl.BlockSpec(memory_space=pl.ANY)
    scaled, ends, wide = call(
        end_kernel,
        "ends",
        [
            shaped((4 * 2 * STATE, rows)),
            shaped((STREAMS,) + channels),
            shaped((STREAMS, length * STATE, LANES)),
        ],
        [WHOLE] * 6 + [later],
    )(bc, bc_far, weigh, c, decay, drive * keeps[0, 0:1, 0:1], z)

    def local(s, after):
        fetched = s == 1
        return call(
            functools.partial(local_kernel, s),
            "local",
            [shaped((length, inner)), shaped((length, CHUNK * STATE), bf16)]
            + [shaped((inner, width), bf16)] * fetched,
            [WHOLE] * 6 + [later] + [ANYWHERE] * fetched,
            [pltpu.VMEM((length * STATE, inner), bf16)] + [pltpu.SemaphoreType.DMA] * fetched,
            megabytes=12,
        )(scaled, wide, c, decay, drive.astype(bf16), skip, after, *[in_hbm(w_out)] * fetched)

    got = swap(ends.astype(bf16), "seq", 2)
    strides, powers, first_step, leads = call(
        factor_kernel,
        "factors",
        [
            shaped((2,) + channels),
            shaped((CHUNK * STATE, inner), bf16),
            shaped((2, STREAMS) + channels),
            shaped((max(pairs - 1, 1), STREAMS) + channels),
        ],
        [WHOLE] * 2 + [later],
    )(rate, keeps, scaled)
    y_f, readout_f = local(0, scaled)
    arrived = []
    if pairs > 1:
        sends = call(
            pair_kernel,
            "pairs",
            [shaped(channels, bf16)] * (pairs - 1),
            [WHOLE] * 3 + [later],
        )(ends, got, first_step, y_f)
        arrived = [swap(send, "seq", 4 * m) for m, send in enumerate(sends, 1)]
    y_b, readout_b, out_w = local(1, sends[0] if pairs > 1 else got)

    def finish(same, dtype):
        return call(
            functools.partial(finish_kernel, same),
            "finish",
            [shaped((rows, width // 2), dtype), shaped((STREAMS, rows, inner), bf16)],
            [WHOLE] * (10 + len(arrived)),
        )(powers, strides, got, leads, y_f, y_b, readout_f, readout_b, z, out_w, *arrived)

    def rest(gated, dtype, after):
        return call(
            rest_kernel, "rest", shaped((rows, width // 2), dtype), [WHOLE] * 2 + [later]
        )(gated, out_w, after)

    send, gated_far = finish(False, bf16)
    came = swap(send, "seq", 1)
    keep, gated_own = finish(True, f32)
    first = keep + came.astype(f32)
    sent = first.astype(bf16)
    if ch_count == 2:
        came = swap(sent, "ch", 1)
    second = swap(rest(gated_far, bf16, sent), "seq", 1)
    second = rest(gated_own, f32, sent) + second.astype(f32)
    if ch_count == 2:
        return (second + came.astype(f32)).astype(bf16)
    total = jnp.concatenate([first, second], axis=1)
    return lax.psum_scatter(total.astype(bf16), "ch", scatter_dimension=1, tiled=True)


def solution(mesh):
    placed = (
        P("seq", "ch"),
        P(),
        P(),
        P(),
        P(),
        P(None, None, "ch"),
        P(None, "ch"),
        P("ch"),
        P(None, "ch"),
        P(None, "ch"),
        P("ch"),
        P("ch", None),
    )
    return jax.shard_map(
        body, mesh=mesh, in_specs=placed, out_specs=P("seq", "ch"), check_vma=False
    )
```

```python
import functools

import jax
import jax.numpy as jnp
from jax import lax
from jax.experimental import pallas as pl
from jax.experimental.pallas import tpu as pltpu
from jax.sharding import PartitionSpec as P

CONV = 4
STATE = 16
EDGE = 16
LANES = 128
SUBS = 8
STREAMS = 2
CHUNK = 16
BLOCK = 256
HALVES = 2
epsilon = 1e-05
f32 = jnp.float32
bf16 = jnp.bfloat16

WHOLE = pl.BlockSpec(memory_space=pltpu.VMEM)
SCALARS = pl.BlockSpec(memory_space=pltpu.SMEM)
ANYWHERE = pl.BlockSpec(memory_space=pltpu.HBM)


def shaped(shape, dtype=f32):
    return jax.ShapeDtypeStruct(shape, dtype)


def call(kernel, name, outs, ins, scratch=(), megabytes=4):
    return pl.pallas_call(
        kernel,
        out_shape=outs,
        in_specs=ins,
        out_specs=jax.tree.map(lambda _: WHOLE, outs),
        scratch_shapes=list(scratch),
        compiler_params=pltpu.CompilerParams(vmem_limit_bytes=megabytes << 20),
        name=name,
    )


def tile(t):
    return slice(t * LANES, (t + 1) * LANES)


def spot():
    place = lax.axis_index("seq")
    return place, place & 1, place >> 1


def swap(block, axis, apart):
    count = lax.axis_size(axis)
    return lax.ppermute(block, axis, [(i, i ^ apart) for i in range(count)])


def in_hbm(array):
    return pltpu.with_memory_space_constraint(array, pltpu.HBM)


def both_halves(block):
    if lax.axis_size("ch") == 2:
        return block, swap(block, "ch", 1)
    full = lax.all_gather(block, "ch", axis=1, tiled=True)
    half = full.shape[1] // 2
    return full[:, :half], full[:, half:]


def rims(rim):
    seq_count, ch_count = lax.axis_size("seq"), lax.axis_size("ch")
    pairs = [(i, i + 1) for i in range(1, seq_count - 1, 2)]
    pairs = pairs + [(j, i) for i, j in pairs]
    if ch_count != 2:
        return both_halves(lax.ppermute(rim, "seq", pairs))
    return tuple(
        lax.ppermute(
            rim,
            ("seq", "ch"),
            [(i * ch_count + (k ^ apart), j * ch_count + k) for i, j in pairs for k in range(2)],
        )
        for apart in range(2)
    )


def cut_kernel(hidden, own, rim, sems):
    low = pl.multiple_of(spot()[1] * (own.shape[0] - EDGE), EDGE)
    copies = [
        pltpu.make_async_copy(hidden, own, sems.at[0]),
        pltpu.make_async_copy(hidden.at[pl.ds(low, EDGE), :], rim, sems.at[1]),
    ]
    for copy in copies:
        copy.start()
    for copy in copies:
        copy.wait()


def between(chip, m):
    pair = chip >> 1
    other = pair ^ m
    below = other < pair
    return jnp.where(below, 2 * other + 2, chip + 1), jnp.where(below, chip, 2 * other), below


def init_kernel(
    bounds, tokens_all, w_in, conv_w, conv_b, proj, rate_all, skip, gain_all, embed_all, after,
    signal_w, taps, offset, proj_half, rate, skip_half, norm_gain, embed,
    bases, weigh, decay, keeps, tokens, sems,
):
    place, core, chip = spot()
    count, rows = tokens.shape
    length = 2 * rows
    inner = signal_w.shape[1]
    chips = count // 2
    mine = pl.ds(pl.multiple_of(core * inner, inner), inner)
    copies = [
        pltpu.make_async_copy(source, target, sems.at[i])
        for i, (source, target) in enumerate(
            (
                (rate_all.at[:, mine], rate),
                (tokens_all, tokens),
                (gain_all, norm_gain),
                (embed_all, embed),
                (conv_w.at[:, mine], taps),
                (conv_b.at[:, mine], offset),
                (proj.at[:, mine], proj_half),
                (skip.at[:, mine], skip_half),
                (w_in.at[0, :, mine], signal_w),
            )
        )
    ]
    for copy in copies:
        copy.start()

    marks = [bounds[k, i] for i in range(bounds.shape[1]) for k in range(2)]
    factors = []
    for i, mark in enumerate(marks):
        total = jnp.int32(1)
        earlier = jnp.int32(0)
        for k, other in enumerate(marks):
            same = jnp.where(other == mark, 1, 0)
            total = total + same
            if k < i:
                earlier = earlier + same
        factors.append(jnp.where(earlier > 0, 1, total).astype(f32))

    start = chip * length
    at = lax.broadcasted_iota(jnp.int32, (SUBS, rows), 1) + start
    for half in range(HALVES):
        runs = [jnp.ones((SUBS, rows), f32) for _ in range(STREAMS)]
        for mark, factor in zip(marks, factors):
            here = at + half * rows
            runs[0] = runs[0] * jnp.where((here >= mark) & (mark >= start), factor, 1.0)
            runs[1] = runs[1] * jnp.where((here <= mark) & (mark < start + length), factor, 1.0)
        for s in range(STREAMS):
            first = 2 * STATE * (2 * half + s)
            for k in range(STATE // SUBS):
                weigh[first + k * SUBS : first + (k + 1) * SUBS, :] = runs[s]
                low = first + STATE + k * SUBS
                weigh[low : low + SUBS, :] = 1.0 / runs[s]

    def kept(low, high):
        total = jnp.ones((SUBS, LANES), f32)
        for mark, factor in zip(marks, factors):
            total = total * jnp.where(
                (mark >= low * length) & (mark < high * length), factor, 1.0
            )
        return 1.0 / total

    keeps[0] = kept(chip, chip + 1)
    keeps[1] = kept(chip ^ 1, (chip ^ 1) + 1)
    for m in range(1, chips // 2):
        low, high, _ = between(chip, m)
        keeps[1 + m] = kept(low, high)
    copies[0].wait()
    for t in range(inner // LANES):
        decay[:, tile(t)] = jnp.exp(-rate[:, tile(t)])

    copies[1].wait()

    def column(row):
        line = tokens[pl.ds(row, 1), :].astype(f32)
        return jnp.broadcast_to(line, (rows, rows)).T

    bases[:rows, :] = column(place)
    beyond = column(jnp.clip(jnp.where(core == 0, place - 1, place + 1), 0, count - 1))
    beyond = jnp.where(core == 0, beyond[rows - EDGE :], beyond[:EDGE])
    inside = jnp.where(core == 0, place > 0, place < count - 1)
    bases[rows:, :] = jnp.where(inside, beyond, -1.0)
    for copy in copies[2:]:
        copy.wait()


def norm_kernel(own, far, own_rim, far_rim, bases, gain, embed, out):
    rows = own.shape[0]
    half = own.shape[1]
    index = lax.axis_index("ch") if lax.axis_size("ch") == 2 else jnp.int32(0)

    def one(first, second, low, count):
        marks = bases[low : low + count, :]
        total = jnp.zeros((count, LANES), f32)
        for part in (first, second):
            for t in range(half // LANES):
                v = part[:, tile(t)].astype(f32)
                total = total + v * v
        inv_rms = lax.rsqrt(jnp.sum(total, axis=1, keepdims=True) / (2 * half) + epsilon)
        inv_rms = jnp.broadcast_to(inv_rms, (count, LANES))
        for k, part in enumerate((first, second)):
            for t in range(half // LANES):
                cols = slice(k * half + t * LANES, k * half + (t + 1) * LANES)
                e = [embed[b : b + 1, cols] for b in range(4)]
                added = jnp.where(
                    marks < 0.5, e[0], jnp.where(marks < 1.5, e[1], jnp.where(marks < 2.5, e[2], e[3]))
                )
                v = part[:, tile(t)].astype(f32) * inv_rms * gain[0:1, cols] + added
                out[low : low + count, cols] = jnp.where(marks < -0.5, 0.0, v).astype(bf16)

    @pl.when(index == 0)
    def _():
        one(own, far, 0, rows)
        one(own_rim, far_rim, rows, EDGE)

    @pl.when(index != 0)
    def _():
        one(far, own, 0, rows)
        one(far_rim, own_rim, rows, EDGE)


def signal_kernel(
    own, other, w, taps, offset, proj, w_in, lined, c_out, bc_out, gate_w, x_tiles, sem
):
    _, core, _ = spot()
    rows = own.shape[0] - EDGE
    length = 2 * rows
    width = own.shape[1]
    padded = length + EDGE
    inner = w.shape[1]
    block = min(BLOCK, inner)
    tiles = block // LANES
    fetch = pltpu.make_async_copy(
        w_in.at[1, :, pl.ds(pl.multiple_of(core * inner, inner), inner)], gate_w, sem
    )
    fetch.start()

    def line_up(first, second):
        lined[0:EDGE, :] = first[rows:, :]
        lined[EDGE : EDGE + rows, :] = first[:rows, :]
        lined[EDGE + rows : padded, :] = second[:rows, :]
        r = lax.broadcasted_iota(jnp.int32, (LANES, LANES), 0)
        q = lax.broadcasted_iota(jnp.int32, (LANES, LANES), 1)
        turn = jnp.where(r + q == LANES - 1, 1.0, 0.0).astype(bf16)
        for t in range(width // LANES):
            at = tile(width // LANES - 1 - t)
            for base, piece in ((0, first[:rows, at]), (rows, second[:, at])):
                turned = jnp.dot(piece, turn, preferred_element_type=f32).astype(bf16)
                lined[padded + base : padded + base + piece.shape[0], tile(t)] = turned

    @pl.when(core == 0)
    def _():
        line_up(own, other)

    @pl.when(core != 0)
    def _():
        line_up(other, own)

    inner_bc = 2 * STATE
    sums = [jnp.zeros((inner_bc, rows), f32) for _ in range(STREAMS * HALVES)]

    def project(b, s):
        x = jnp.dot(
            lined[s * padded : (s + 1) * padded, :],
            w[:, b * block : (b + 1) * block],
            preferred_element_type=f32,
        )
        x = x.astype(bf16).astype(f32)
        for t in range(tiles):
            x_tiles[(b % 2 * STREAMS + s) * tiles + t] = x[:, tile(t)]

    def convolve(b, s):
        mixed = []
        for t in range(tiles):
            slot = (b % 2 * STREAMS + s) * tiles + t
            cols = tile(b * tiles + t)
            total = offset[0:1, cols]
            for k in range(CONV):
                at = EDGE - CONV + 1 + k if s == 0 else CONV - 1 - k
                total = total + x_tiles[slot, at : at + length, :] * taps[k : k + 1, cols]
            c = jax.nn.silu(total).astype(bf16)
            c_out[s, b * tiles + t] = c.astype(f32)
            mixed.append(c)
        mixed = mixed[0] if tiles == 1 else jnp.concatenate(mixed, axis=1)
        for half in range(HALVES):
            sums[2 * half + s] = sums[2 * half + s] + lax.dot_general(
                proj[:, b * block : (b + 1) * block],
                mixed[half * rows : (half + 1) * rows],
                (((1,), (1,)), ((), ())),
                preferred_element_type=f32,
            )

    turns = [(b, s) for b in range(inner // block) for s in range(STREAMS)]
    project(*turns[0])
    for before, after in zip(turns, turns[1:] + [None]):
        if after is not None:
            project(*after)
        convolve(*before)
    for i, total in enumerate(sums):
        bc_out[i * inner_bc : (i + 1) * inner_bc, :] = total
    fetch.wait()


def gate_kernel(lined, w, z_out):
    padded = lined.shape[0] // 2
    length = padded - EDGE
    inner = w.shape[1]
    block = min(BLOCK, inner)
    for b in range(inner // block):
        cols = slice(b * block, (b + 1) * block)
        for s, first in ((0, EDGE), (1, padded)):
            z = jnp.dot(lined[first : first + length, :], w[:, cols], preferred_element_type=f32)
            z_out[s, :, cols] = z.astype(bf16)


def lane_of(values, lane):
    return jnp.take_along_axis(values, jnp.full(values.shape, lane, jnp.int32), axis=1)


def tiles_of(ref, count):
    return [ref[h * SUBS : (h + 1) * SUBS, tile(t)] for t in range(count) for h in range(2)]


def spread(bc, wide, stream):
    rows = bc.shape[1]
    ones = jnp.ones((rows, LANES), bf16)
    lanes = lax.broadcasted_iota(jnp.int32, (STATE, rows), 1)
    group = 8
    for half in range(HALVES):
        first = 2 * STATE * (2 * half + stream)
        entries = bc[first : first + STATE, :]
        for j in range(0, rows, group):
            alone = jnp.concatenate(
                [jnp.where(lanes == j + i, entries, 0.0).astype(bf16) for i in range(group)], axis=0
            )
            at = (half * rows + j) * STATE
            wide[stream, at : at + group * STATE, :] = jnp.dot(
                alone, ones, preferred_element_type=f32
            )


def end_kernel(
    bc_own, bc_far, weigh, c, decay, drive, keeps, after_z, w,
    bc_out, end_out, starts, w_out, wide, sem,
):
    inner = w_out.shape[0]
    mine = pl.ds(pl.multiple_of(spot()[1] * inner, inner), inner)
    fetch = pltpu.make_async_copy(w.at[mine, :], w_out, sem)
    fetch.start()
    rows = bc_own.shape[1]
    length = 2 * rows
    count = c.shape[1]
    bc_out[...] = (bc_own[...] + bc_far[...]) * weigh[...]
    for s in range(STREAMS):
        spread(bc_out, wide, s)
    a = tiles_of(decay, count)

    def chunk(n, state):
        for s in range(STREAMS):
            for t in range(count):
                for h in range(2):
                    sub = slice(h * SUBS, (h + 1) * SUBS)
                    starts[s, n, sub, tile(t)] = (
                        state[s * 2 * count + 2 * t + h] * drive[sub, tile(t)]
                    )
        for j in range(CHUNK):
            after = []
            for s in range(STREAMS):
                t0 = n * CHUNK + j if s == 0 else length - 1 - n * CHUNK - j
                low = pl.multiple_of(t0 * STATE, STATE)
                b = [wide[s, pl.ds(low + h * SUBS, SUBS), :] for h in range(2)]
                for t in range(count):
                    x = c[s, t, pl.ds(t0, 1), :]
                    for h in range(2):
                        i = 2 * t + h
                        after.append(a[i] * state[s * 2 * count + i] + b[h] * x)
            state = tuple(after)
        return state

    zero = jnp.zeros((SUBS, LANES), f32)
    state = lax.fori_loop(0, length // CHUNK, chunk, (zero,) * (STREAMS * 2 * count))
    for s in range(STREAMS):
        for t in range(count):
            for h in range(2):
                sub = slice(h * SUBS, (h + 1) * SUBS)
                end_out[s, sub, tile(t)] = (
                    state[s * 2 * count + 2 * t + h] * drive[sub, tile(t)] * keeps[0, 0:1, :]
                )
    fetch.wait()


def local_kernel(
    stream, bc, c, decay, drive, skip, after, y_out, readout, lined, c_lined, y_lined
):
    rows = bc.shape[1]
    length = 2 * rows
    count = c.shape[1]
    span = CHUNK * STATE
    places = length // CHUNK
    turned = bc[...].T
    r = lax.broadcasted_iota(jnp.int32, (rows, span), 0)
    q = lax.broadcasted_iota(jnp.int32, (rows, span), 1)
    step = r & (CHUNK - 1) if stream == 0 else CHUNK - 1 - (r & (CHUNK - 1))
    for half in range(HALVES):
        column = 2 * STATE * (2 * half + stream)
        pick = jnp.where(r == column + STATE + (q & (STATE - 1)), 1.0, 0.0).astype(bf16)
        picked = jnp.dot(turned.astype(bf16), pick, preferred_element_type=f32)
        readout[half * rows : (half + 1) * rows, :] = jnp.where(
            q // STATE == step, picked, 0.0
        ).astype(bf16)
        lined[0, half * rows : (half + 1) * rows, :] = (
            turned if column == 0 else pltpu.roll(turned, LANES - column, 1)
        )
    for j in range(CHUNK):
        to = slice(j * places, (j + 1) * places)
        lined[1, to, :] = lined[0, pl.ds(j, places, stride=CHUNK), :]
        for t in range(count):
            c_lined[t, to, :] = c[stream, t, pl.ds(j, places, stride=CHUNK), :]
    inputs = lined[1]
    outputs = pltpu.roll(inputs, LANES - STATE, 1)
    block = min(2, count)
    for low in range(0, count, block):
        wide = slice(low * LANES, (low + block) * LANES)
        reach = drive[:, wide]
        for lag in range(CHUNK):
            shift = lag * places
            near, far = slice(shift, length), slice(0, length - shift)
            if stream == 1:
                near, far = far, near
            left = (outputs[near] * inputs[far])[:, :STATE].astype(bf16)
            found = jnp.dot(left, reach.astype(bf16), preferred_element_type=f32)
            for t in range(block):
                part = found[:, tile(t)]
                if lag == 0:
                    part = part + skip[0:1, tile(low + t)]
                part = part * c_lined[low + t, far, :]
                if lag == 0:
                    y_lined[low + t, near, :] = part
                else:
                    y_lined[low + t, near, :] += part
            reach = reach * decay[:, wide]
    for j in range(CHUNK):
        at = slice(j * places, (j + 1) * places)
        for t in range(count):
            y_out[t, pl.ds(j, places, stride=CHUNK), :] = y_lined[t, at, :]


def factor_kernel(rate, keeps, after_ends, strides, powers, first_step, leads):
    _, _, chip = spot()
    inner = rate.shape[1]
    upper = chip & 1
    for t in range(inner // LANES):
        d = rate[:, tile(t)]
        a = jnp.exp(-d)
        strides[0, :, tile(t)] = jnp.exp(-float(CHUNK) * d)
        strides[1, :, tile(t)] = jnp.exp(-float(LANES) * d)
        power = a
        for j in range(CHUNK):
            powers[j * STATE : (j + 1) * STATE, tile(t)] = power.astype(bf16)
            power = power * a
        d = d * float(-2 * LANES)
        span = jnp.exp(d)
        own = span * keeps[0, 0:1, :]
        beside = span * keeps[1, 0:1, :]
        first_step[0, 0, :, tile(t)] = jnp.where(upper == 1, own, 1.0)
        first_step[0, 1, :, tile(t)] = jnp.where(upper == 1, 1.0, own)
        first_step[1, 0, :, tile(t)] = jnp.where(upper == 1, 1.0, beside)
        first_step[1, 1, :, tile(t)] = jnp.where(upper == 1, beside, 1.0)
        for m in range(1, keeps.shape[0] - 1):
            low, high, below = between(chip, m)
            lead = jnp.exp(d * (high - low).astype(f32)) * keeps[1 + m, 0:1, :]
            leads[m - 1, 0, :, tile(t)] = jnp.where(below, lead, 0.0)
            leads[m - 1, 1, :, tile(t)] = jnp.where(below, 0.0, lead)


def pair_kernel(ends, got, first_step, after_local, *sends):
    _, _, chip = spot()
    group = [
        (got[s].astype(f32) * first_step[0, s] + ends[s] * first_step[1, s]).astype(bf16)
        for s in range(STREAMS)
    ]
    for m, send in enumerate(sends):
        _, _, below = between(chip, m + 1)
        send[...] = jnp.where(below, group[1], group[0])


def columns(gated, w, out, part):
    inner, width = w.shape
    rows, half = out.shape
    base = pl.multiple_of(part * half, half)
    back = LANES - 1 - lax.broadcasted_iota(jnp.int32, (rows, LANES), 1)
    strip = min(BLOCK, half)
    for low in range(0, half, strip):
        here = pl.ds(pl.multiple_of(base + low, strip), strip)
        there = pl.ds(pl.multiple_of(width - base - low - strip, strip), strip)
        ahead = jnp.dot(gated[0], w[:, here], preferred_element_type=f32)
        behind = jnp.dot(gated[1], w[:, there], preferred_element_type=f32)
        for t in range(strip // LANES):
            turned = jnp.take_along_axis(behind[:, tile(strip // LANES - 1 - t)], back, axis=1)
            total = ahead[:, tile(t)] + turned
            out[:, low + t * LANES : low + (t + 1) * LANES] = total.astype(out.dtype)


def part_of(own):
    if lax.axis_size("ch") != 2:
        return jnp.int32(1 if own else 0)
    return lax.axis_index("ch") if own else 1 - lax.axis_index("ch")


def finish_kernel(
    same, powers, strides, got, leads, starts, y_f, y_b, readout_f, readout_b, z, w, *rest
):
    if same:
        *arrived, out, gated = rest
    else:
        *arrived, out, out_rest, gated = rest
    _, core, chip = spot()
    rows = out.shape[0]
    inner = w.shape[0]
    half = core if same else 1 - core
    base = pl.multiple_of(half * rows, rows)
    span = CHUNK * STATE
    local = (y_f, y_b)
    readouts = (readout_f, readout_b)
    for s in range(STREAMS):
        state = got[s].astype(f32) * jnp.where(chip & 1 == 1 - s, 1.0, 0.0)
        for m, part in enumerate(arrived):
            state = state + part[...].astype(f32) * leads[m, s]
        late = half == 1 - s
        state = state * jnp.where(late, strides[1], 1.0)
        first = jnp.where(late, rows // CHUNK, 0)
        for q in range(rows // CHUNK):
            row = q * CHUNK if s == 0 else rows - (q + 1) * CHUNK
            at = pl.ds(pl.multiple_of(base + row, CHUNK), CHUNK)
            begin = (state + starts[s, first + q]).astype(bf16)
            carried = powers[...].reshape(CHUNK, STATE, inner) * begin[None]
            state = state * strides[0]
            y = jnp.dot(
                readouts[s][at, :], carried.reshape(span, inner), preferred_element_type=f32
            )
            for t in range(inner // LANES):
                gated[s, row : row + CHUNK, tile(t)] = (
                    (y[:, tile(t)] + local[s][t, at, :])
                    * jax.nn.silu(z[s, at, tile(t)].astype(f32))
                ).astype(bf16)
    columns(gated, w, out, part_of(False))
    if not same:
        columns(gated, w, out_rest, part_of(True))


def rest_kernel(gated, w, after_first, out):
    columns(gated, w, out, part_of(True))


def body(
    hidden,
    tokens,
    edit_bounds,
    norm_gain,
    base_embed,
    w_in,
    conv_w,
    conv_b,
    proj_bc,
    decay_rate,
    skip_gain,
    w_out,
):
    rows = hidden.shape[0]
    width = w_in.shape[1]
    inner = w_in.shape[2] // 2
    tiles = inner // LANES
    length = 2 * rows
    padded = length + EDGE
    block = min(BLOCK, inner)
    seq_count = lax.axis_size("seq")
    ch_count = lax.axis_size("ch")
    chips = seq_count // 2
    chip = spot()[2]

    own, rim = call(
        cut_kernel,
        "cut",
        [shaped(hidden.shape, bf16), shaped((EDGE, hidden.shape[1]), bf16)],
        [ANYWHERE],
        [pltpu.SemaphoreType.DMA((2,))],
    )(in_hbm(hidden))
    later = pl.BlockSpec(memory_space=pl.ANY)
    rim_first, rim_second = rims(rim)
    first, second = both_halves(own)
    channels = (STATE, inner)
    pairs = chips // 2
    (
        signal_w, taps, offset, proj_half, rate, skip, gain, embed,
        bases, weigh, decay, keeps,
    ) = call(
        init_kernel,
        "init",
        [
            shaped((width, inner), bf16),
            shaped((CONV, inner)),
            shaped((1, inner)),
            shaped((2 * STATE, inner), bf16),
            shaped(channels),
            shaped((1, inner)),
            shaped((1, width)),
            shaped((4, width)),
            shaped((rows + EDGE, LANES)),
            shaped((4 * 2 * STATE, rows)),
            shaped(channels),
            shaped((max(pairs, 1) + 1, SUBS, LANES)),
        ],
        [SCALARS] + [ANYWHERE] * 9 + [later],
        [pltpu.VMEM((seq_count, rows), jnp.int32), pltpu.SemaphoreType.DMA((9,))],
    )(
        edit_bounds.T,
        *(
            in_hbm(array)
            for array in (
                tokens.reshape(seq_count, rows),
                w_in,
                conv_w,
                conv_b[None, :],
                proj_bc,
                decay_rate,
                skip_gain[None, :],
                norm_gain[None, :],
                base_embed,
            )
        ),
        rim,
    )
    drive = jnp.sqrt(-jnp.expm1(-2.0 * rate))
    normed = call(norm_kernel, "norm", shaped((rows + EDGE, width), bf16), [WHOLE] * 7)(
        first, second, rim_first, rim_second, bases, gain, embed
    )
    partner = swap(normed, "seq", 1)

    lined, c, bc, gate_w = call(
        signal_kernel,
        "signal",
        [
            shaped((2 * padded, width), bf16),
            shaped((STREAMS, tiles, length, LANES)),
            shaped((4 * 2 * STATE, rows)),
            shaped((width, inner), bf16),
        ],
        [WHOLE] * 6 + [ANYWHERE],
        [
            pltpu.VMEM((2 * STREAMS * block // LANES, padded, LANES), f32),
            pltpu.SemaphoreType.DMA,
        ],
        megabytes=6,
    )(normed, partner, signal_w, taps, offset, proj_half, in_hbm(w_in))
    bc = bc + swap(bc, "seq", 1)
    if ch_count == 2:
        bc_far = swap(bc, "ch", 1)
    else:
        bc, bc_far = lax.psum(bc, "ch"), jnp.zeros_like(bc)

    z = call(gate_kernel, "gate", shaped((STREAMS, length, inner), bf16), [WHOLE] * 2)(
        lined, gate_w
    )
    scaled, ends, starts, out_w = call(
        end_kernel,
        "ends",
        [
            shaped((4 * 2 * STATE, rows)),
            shaped((STREAMS,) + channels),
            shaped((STREAMS, length // CHUNK) + channels),
            shaped((inner, width), bf16),
        ],
        [WHOLE] * 7 + [later, ANYWHERE],
        [pltpu.VMEM((STREAMS, length * STATE, LANES), f32), pltpu.SemaphoreType.DMA],
        megabytes=6,
    )(bc, bc_far, weigh, c, decay, drive, keeps, z, in_hbm(w_out))

    got = swap(ends.astype(bf16), "seq", 2)
    strides, powers, first_step, leads = call(
        factor_kernel,
        "factors",
        [
            shaped((2,) + channels),
            shaped((CHUNK * STATE, inner), bf16),
            shaped((2, STREAMS) + channels),
            shaped((max(pairs - 1, 1), STREAMS) + channels),
        ],
        [WHOLE] * 2 + [later],
    )(rate, keeps, scaled)
    by_tile = (tiles, length, LANES)

    def local(s, after):
        return call(
            functools.partial(local_kernel, s),
            "local",
            [shaped(by_tile), shaped((length, CHUNK * STATE), bf16)],
            [WHOLE] * 5 + [later],
            [
                pltpu.VMEM((2, length, LANES), f32),
                pltpu.VMEM(by_tile, f32),
                pltpu.VMEM(by_tile, f32),
            ],
            megabytes=6,
        )(scaled, c, decay, drive, skip, after)

    y_f, readout_f = local(0, ends)
    arrived = []
    if pairs > 1:
        sends = call(
            pair_kernel,
            "pairs",
            [shaped(channels, bf16)] * (pairs - 1),
            [WHOLE] * 3 + [later],
        )(ends, got, first_step, y_f)
        arrived = [swap(send, "seq", 4 * m) for m, send in enumerate(sends, 1)]
    y_b, readout_b = local(1, sends[0] if pairs > 1 else got)

    operands = (
        powers, strides, got, leads, starts, y_f, y_b, readout_f, readout_b, z, out_w, *arrived
    )
    half_width = (rows, width // 2)
    gated = (STREAMS, rows, inner)
    both = call(
        functools.partial(finish_kernel, False),
        "finish",
        [shaped(half_width, bf16)] * 2,
        [WHOLE] * len(operands),
        [pltpu.VMEM(gated, bf16)],
    )(*operands)
    first_far, second_far = [swap(send, "seq", 1) for send in both]
    first, gated_own = call(
        functools.partial(finish_kernel, True),
        "finish",
        [shaped(half_width), shaped(gated, bf16)],
        [WHOLE] * len(operands),
    )(*operands)
    first = first + first_far.astype(f32)
    sent = first.astype(bf16)
    if ch_count == 2:
        came = swap(sent, "ch", 1)
    second = call(rest_kernel, "rest", shaped(half_width), [WHOLE] * 2 + [later])(
        gated_own, out_w, sent
    )
    second = second + second_far.astype(f32)
    if ch_count == 2:
        return (second + came.astype(f32)).astype(bf16)
    total = jnp.concatenate([first, second], axis=1)
    return lax.psum_scatter(total.astype(bf16), "ch", scatter_dimension=1, tiled=True)


def solution(mesh):
    placed = (
        P("seq", "ch"),
        P(),
        P(),
        P(),
        P(),
        P(None, None, "ch"),
        P(None, "ch"),
        P("ch"),
        P(None, "ch"),
        P(None, "ch"),
        P("ch"),
        P("ch", None),
    )
    return jax.shard_map(
        body, mesh=mesh, in_specs=placed, out_specs=P("seq", "ch"), check_vma=False
    )
```

```python
import functools

import jax
import jax.numpy as jnp
from jax import lax
from jax.experimental import pallas as pl
from jax.experimental.pallas import tpu as pltpu
from jax.sharding import PartitionSpec as P

CONV = 4
STATE = 16
EDGE = 16
LANES = 128
SUBS = 8
STREAMS = 2
CHUNK = 16
BLOCK = 256
HALVES = 2
epsilon = 1e-05
f32 = jnp.float32
bf16 = jnp.bfloat16

WHOLE = pl.BlockSpec(memory_space=pltpu.VMEM)
SCALARS = pl.BlockSpec(memory_space=pltpu.SMEM)
ANYWHERE = pl.BlockSpec(memory_space=pltpu.HBM)


def shaped(shape, dtype=f32):
    return jax.ShapeDtypeStruct(shape, dtype)


def call(kernel, name, outs, ins, scratch=(), megabytes=4):
    return pl.pallas_call(
        kernel,
        out_shape=outs,
        in_specs=ins,
        out_specs=jax.tree.map(lambda _: WHOLE, outs),
        scratch_shapes=list(scratch),
        compiler_params=pltpu.CompilerParams(vmem_limit_bytes=megabytes << 20),
        name=name,
    )


def tile(t):
    return slice(t * LANES, (t + 1) * LANES)


def spot():
    place = lax.axis_index("seq")
    return place, place & 1, place >> 1


def swap(block, axis, apart):
    count = lax.axis_size(axis)
    return lax.ppermute(block, axis, [(i, i ^ apart) for i in range(count)])


def in_hbm(array):
    return pltpu.with_memory_space_constraint(array, pltpu.HBM)


def both_halves(block):
    if lax.axis_size("ch") == 2:
        return block, swap(block, "ch", 1)
    full = lax.all_gather(block, "ch", axis=1, tiled=True)
    half = full.shape[1] // 2
    return full[:, :half], full[:, half:]


def rims(rim):
    seq_count, ch_count = lax.axis_size("seq"), lax.axis_size("ch")
    pairs = [(i, i + 1) for i in range(1, seq_count - 1, 2)]
    pairs = pairs + [(j, i) for i, j in pairs]
    if ch_count != 2:
        return both_halves(lax.ppermute(rim, "seq", pairs))
    return tuple(
        lax.ppermute(
            rim,
            ("seq", "ch"),
            [(i * ch_count + (k ^ apart), j * ch_count + k) for i, j in pairs for k in range(2)],
        )
        for apart in range(2)
    )


def rim_kernel(hidden, rim, sem):
    low = pl.multiple_of(spot()[1] * (hidden.shape[0] - EDGE), EDGE)
    copy = pltpu.make_async_copy(hidden.at[pl.ds(low, EDGE), :], rim, sem)
    copy.start()
    copy.wait()


def between(chip, m):
    pair = chip >> 1
    other = pair ^ m
    below = other < pair
    return jnp.where(below, 2 * other + 2, chip + 1), jnp.where(below, chip, 2 * other), below


def init_kernel(
    bounds_all, tokens_all, w_in, conv_w, conv_b, proj, rate_all, skip, gain_all, embed_all, after,
    signal_w, gate_w, taps, offset, proj_half, rate, skip_half, norm_gain, embed,
    bases, weigh, decay, keeps, bounds, tokens, sems,
):
    place, core, chip = spot()
    count, rows = tokens.shape
    length = 2 * rows
    inner = rate.shape[1]
    chips = count // 2
    mine = pl.ds(pl.multiple_of(core * inner, inner), inner)
    copies = [
        pltpu.make_async_copy(source, target, sems.at[i])
        for i, (source, target) in enumerate(
            (
                (bounds_all, bounds),
                (rate_all.at[:, mine], rate),
                (tokens_all, tokens),
                (gain_all, norm_gain),
                (embed_all, embed),
                (conv_w.at[:, mine], taps),
                (conv_b.at[:, mine], offset),
                (proj.at[:, mine], proj_half),
                (skip.at[:, mine], skip_half),
                (w_in.at[0, :, mine], signal_w),
                (w_in.at[1, :, mine], gate_w),
            )
        )
    ]
    for copy in copies:
        copy.start()

    copies[0].wait()
    marks = [bounds[k, i] for i in range(bounds.shape[1]) for k in range(2)]
    factors = []
    for i, mark in enumerate(marks):
        total = jnp.int32(1)
        earlier = jnp.int32(0)
        for k, other in enumerate(marks):
            same = jnp.where(other == mark, 1, 0)
            total = total + same
            if k < i:
                earlier = earlier + same
        factors.append(jnp.where(earlier > 0, 1, total).astype(f32))

    start = chip * length
    at = lax.broadcasted_iota(jnp.int32, (SUBS, rows), 1) + start
    for half in range(HALVES):
        runs = [jnp.ones((SUBS, rows), f32) for _ in range(STREAMS)]
        for mark, factor in zip(marks, factors):
            here = at + half * rows
            runs[0] = runs[0] * jnp.where((here >= mark) & (mark >= start), factor, 1.0)
            runs[1] = runs[1] * jnp.where((here <= mark) & (mark < start + length), factor, 1.0)
        for s in range(STREAMS):
            first = 2 * STATE * (2 * half + s)
            for k in range(STATE // SUBS):
                weigh[first + k * SUBS : first + (k + 1) * SUBS, :] = runs[s]
                low = first + STATE + k * SUBS
                weigh[low : low + SUBS, :] = 1.0 / runs[s]

    def kept(low, high):
        total = jnp.ones((SUBS, LANES), f32)
        for mark, factor in zip(marks, factors):
            total = total * jnp.where(
                (mark >= low * length) & (mark < high * length), factor, 1.0
            )
        return 1.0 / total

    keeps[0] = kept(chip, chip + 1)
    keeps[1] = kept(chip ^ 1, (chip ^ 1) + 1)
    for m in range(1, chips // 2):
        low, high, _ = between(chip, m)
        keeps[1 + m] = kept(low, high)
    copies[1].wait()
    for t in range(inner // LANES):
        decay[:, tile(t)] = jnp.exp(-rate[:, tile(t)])

    copies[2].wait()

    def column(row):
        line = tokens[pl.ds(row, 1), :].astype(f32)
        return jnp.broadcast_to(line, (rows, rows)).T

    bases[:rows, :] = column(place)
    beyond = column(jnp.clip(jnp.where(core == 0, place - 1, place + 1), 0, count - 1))
    beyond = jnp.where(core == 0, beyond[rows - EDGE :], beyond[:EDGE])
    inside = jnp.where(core == 0, place > 0, place < count - 1)
    bases[rows:, :] = jnp.where(inside, beyond, -1.0)
    for copy in copies[3:]:
        copy.wait()


def norm_kernel(own, far, own_rim, far_rim, bases, gain, embed, out):
    rows = own.shape[0]
    half = own.shape[1]
    index = lax.axis_index("ch") if lax.axis_size("ch") == 2 else jnp.int32(0)

    def one(first, second, low, count):
        marks = bases[low : low + count, :]
        total = jnp.zeros((count, LANES), f32)
        for part in (first, second):
            for t in range(half // LANES):
                v = part[:, tile(t)].astype(f32)
                total = total + v * v
        inv_rms = lax.rsqrt(jnp.sum(total, axis=1, keepdims=True) / (2 * half) + epsilon)
        inv_rms = jnp.broadcast_to(inv_rms, (count, LANES))
        for k, part in enumerate((first, second)):
            for t in range(half // LANES):
                cols = slice(k * half + t * LANES, k * half + (t + 1) * LANES)
                e = [embed[b : b + 1, cols] for b in range(4)]
                added = jnp.where(
                    marks < 0.5, e[0], jnp.where(marks < 1.5, e[1], jnp.where(marks < 2.5, e[2], e[3]))
                )
                v = part[:, tile(t)].astype(f32) * inv_rms * gain[0:1, cols] + added
                out[low : low + count, cols] = jnp.where(marks < -0.5, 0.0, v).astype(bf16)

    @pl.when(index == 0)
    def _():
        one(own, far, 0, rows)
        one(own_rim, far_rim, rows, EDGE)

    @pl.when(index != 0)
    def _():
        one(far, own, 0, rows)
        one(far_rim, own_rim, rows, EDGE)


def both_ways(normed, lined):
    count, width = normed.shape
    lined[:count, :] = normed[...]
    r = lax.broadcasted_iota(jnp.int32, (LANES, LANES), 0)
    q = lax.broadcasted_iota(jnp.int32, (LANES, LANES), 1)
    turn = jnp.where(r + q == LANES - 1, 1.0, 0.0).astype(bf16)
    for t in range(width // LANES):
        piece = normed[:, tile(width // LANES - 1 - t)]
        lined[count:, tile(t)] = jnp.dot(piece, turn, preferred_element_type=f32).astype(bf16)


def own_signal_kernel(normed, w, lined, x_out):
    inner = w.shape[1]
    block = min(BLOCK, inner)
    both_ways(normed, lined)
    for b in range(inner // block):
        cols = slice(b * block, (b + 1) * block)
        x = jnp.dot(lined[...], w[:, cols], preferred_element_type=f32)
        x_out[:, cols] = x.astype(bf16).astype(f32)


def signal_kernel(
    normed, x_own, w, taps, offset, proj, lined, c_out, bc_out, x_tiles
):
    _, core, _ = spot()
    count = normed.shape[0]
    rows = count - EDGE
    length = 2 * rows
    inner = w.shape[1]
    block = min(BLOCK, inner)
    tiles = block // LANES
    both_ways(normed, lined)
    inner_bc = 2 * STATE
    sums = [jnp.zeros((inner_bc, rows), f32) for _ in range(STREAMS * HALVES)]

    def project(b):
        other = jnp.dot(
            lined[...], w[:, b * block : (b + 1) * block], preferred_element_type=f32
        )
        other = other.astype(bf16).astype(f32)
        for s in range(STREAMS):
            first = EDGE * (1 - s)
            low = s * count
            for t in range(tiles):
                slot = (b % 2 * STREAMS + s) * tiles + t
                mine = x_own[low : low + count, tile(b * tiles + t)]
                far = other[low : low + count, tile(t)]
                x_tiles[slot, first : first + rows, :] = jnp.where(
                    core == 0, mine[:rows], far[:rows]
                )
                x_tiles[slot, first + rows : first + length, :] = jnp.where(
                    core == 0, far[:rows], mine[:rows]
                )
                x_tiles[slot, s * length : s * length + EDGE, :] = jnp.where(
                    core == s, mine[rows:], far[rows:]
                )

    def convolve(b, s):
        mixed = []
        for t in range(tiles):
            slot = (b % 2 * STREAMS + s) * tiles + t
            cols = tile(b * tiles + t)
            total = offset[0:1, cols]
            for k in range(CONV):
                at = EDGE - CONV + 1 + k if s == 0 else CONV - 1 - k
                total = total + x_tiles[slot, at : at + length, :] * taps[k : k + 1, cols]
            c = jax.nn.silu(total).astype(bf16)
            c_out[s, b * tiles + t] = c.astype(f32)
            mixed.append(c)
        mixed = mixed[0] if tiles == 1 else jnp.concatenate(mixed, axis=1)
        for half in range(HALVES):
            sums[2 * half + s] = sums[2 * half + s] + lax.dot_general(
                proj[:, b * block : (b + 1) * block],
                mixed[half * rows : (half + 1) * rows],
                (((1,), (1,)), ((), ())),
                preferred_element_type=f32,
            )

    blocks = inner // block
    project(0)
    for b in range(blocks):
        if b + 1 < blocks:
            project(b + 1)
        for s in range(STREAMS):
            convolve(b, s)
    for i, total in enumerate(sums):
        bc_out[i * inner_bc : (i + 1) * inner_bc, :] = total


def gate_kernel(lined_own, lined_other, w, z_out):
    _, core, _ = spot()
    count = lined_own.shape[0] // 2
    rows = count - EDGE
    inner = w.shape[1]
    block = min(BLOCK, inner)
    for b in range(inner // block):
        cols = slice(b * block, (b + 1) * block)
        for lined, half in ((lined_own, core), (lined_other, 1 - core)):
            z = jnp.dot(lined[...], w[:, cols], preferred_element_type=f32).astype(bf16)
            at = pl.ds(pl.multiple_of(half * rows, rows), rows)
            for s in range(STREAMS):
                z_out[s, at, cols] = z[s * count : s * count + rows]


def lane_of(values, lane):
    return jnp.take_along_axis(values, jnp.full(values.shape, lane, jnp.int32), axis=1)


def tiles_of(ref, count):
    return [ref[h * SUBS : (h + 1) * SUBS, tile(t)] for t in range(count) for h in range(2)]


def spread(bc, wide, stream):
    rows = bc.shape[1]
    ones = jnp.ones((rows, LANES), bf16)
    lanes = lax.broadcasted_iota(jnp.int32, (STATE, rows), 1)
    group = 8
    for half in range(HALVES):
        first = 2 * STATE * (2 * half + stream)
        entries = bc[first : first + STATE, :]
        for j in range(0, rows, group):
            alone = jnp.concatenate(
                [jnp.where(lanes == j + i, entries, 0.0).astype(bf16) for i in range(group)], axis=0
            )
            at = (half * rows + j) * STATE
            wide[stream, at : at + group * STATE, :] = jnp.dot(
                alone, ones, preferred_element_type=f32
            )


def end_kernel(
    bc_own, bc_far, weigh, c, decay, drive, keeps, after_z, w,
    bc_out, end_out, starts, w_out, wide, sem,
):
    inner = w_out.shape[0]
    mine = pl.ds(pl.multiple_of(spot()[1] * inner, inner), inner)
    fetch = pltpu.make_async_copy(w.at[mine, :], w_out, sem)
    fetch.start()
    rows = bc_own.shape[1]
    length = 2 * rows
    count = c.shape[1]
    bc_out[...] = (bc_own[...] + bc_far[...]) * weigh[...]
    for s in range(STREAMS):
        spread(bc_out, wide, s)
    a = tiles_of(decay, count)

    def chunk(n, state):
        for s in range(STREAMS):
            for t in range(count):
                for h in range(2):
                    sub = slice(h * SUBS, (h + 1) * SUBS)
                    starts[s, n, sub, tile(t)] = (
                        state[s * 2 * count + 2 * t + h] * drive[sub, tile(t)]
                    )
        for j in range(CHUNK):
            after = []
            for s in range(STREAMS):
                t0 = n * CHUNK + j if s == 0 else length - 1 - n * CHUNK - j
                low = pl.multiple_of(t0 * STATE, STATE)
                b = [wide[s, pl.ds(low + h * SUBS, SUBS), :] for h in range(2)]
                for t in range(count):
                    x = c[s, t, pl.ds(t0, 1), :]
                    for h in range(2):
                        i = 2 * t + h
                        after.append(a[i] * state[s * 2 * count + i] + b[h] * x)
            state = tuple(after)
        return state

    zero = jnp.zeros((SUBS, LANES), f32)
    state = lax.fori_loop(0, length // CHUNK, chunk, (zero,) * (STREAMS * 2 * count))
    for s in range(STREAMS):
        for t in range(count):
            for h in range(2):
                sub = slice(h * SUBS, (h + 1) * SUBS)
                end_out[s, sub, tile(t)] = (
                    state[s * 2 * count + 2 * t + h] * drive[sub, tile(t)] * keeps[0, 0:1, :]
                )
    fetch.wait()


def local_kernel(
    stream, bc, c, decay, drive, skip, after, y_out, readout, lined, c_lined, y_lined
):
    rows = bc.shape[1]
    length = 2 * rows
    count = c.shape[1]
    span = CHUNK * STATE
    places = length // CHUNK
    turned = bc[...].T
    r = lax.broadcasted_iota(jnp.int32, (rows, span), 0)
    q = lax.broadcasted_iota(jnp.int32, (rows, span), 1)
    step = r & (CHUNK - 1) if stream == 0 else CHUNK - 1 - (r & (CHUNK - 1))
    for half in range(HALVES):
        column = 2 * STATE * (2 * half + stream)
        pick = jnp.where(r == column + STATE + (q & (STATE - 1)), 1.0, 0.0).astype(bf16)
        picked = jnp.dot(turned.astype(bf16), pick, preferred_element_type=f32)
        readout[half * rows : (half + 1) * rows, :] = jnp.where(
            q // STATE == step, picked, 0.0
        ).astype(bf16)
        lined[0, half * rows : (half + 1) * rows, :] = (
            turned if column == 0 else pltpu.roll(turned, LANES - column, 1)
        )
    for j in range(CHUNK):
        to = slice(j * places, (j + 1) * places)
        lined[1, to, :] = lined[0, pl.ds(j, places, stride=CHUNK), :]
        for t in range(count):
            c_lined[t, to, :] = c[stream, t, pl.ds(j, places, stride=CHUNK), :]
    inputs = lined[1]
    outputs = pltpu.roll(inputs, LANES - STATE, 1)
    block = min(2, count)
    for low in range(0, count, block):
        wide = slice(low * LANES, (low + block) * LANES)
        reach = drive[:, wide]
        for lag in range(CHUNK):
            shift = lag * places
            near, far = slice(shift, length), slice(0, length - shift)
            if stream == 1:
                near, far = far, near
            left = (outputs[near] * inputs[far])[:, :STATE].astype(bf16)
            found = jnp.dot(left, reach.astype(bf16), preferred_element_type=f32)
            for t in range(block):
                part = found[:, tile(t)]
                if lag == 0:
                    part = part + skip[0:1, tile(low + t)]
                part = part * c_lined[low + t, far, :]
                if lag == 0:
                    y_lined[low + t, near, :] = part
                else:
                    y_lined[low + t, near, :] += part
            reach = reach * decay[:, wide]
    for j in range(CHUNK):
        at = slice(j * places, (j + 1) * places)
        for t in range(count):
            y_out[t, pl.ds(j, places, stride=CHUNK), :] = y_lined[t, at, :]


def factor_kernel(rate, keeps, after_ends, strides, powers, first_step, leads):
    _, _, chip = spot()
    inner = rate.shape[1]
    upper = chip & 1
    for t in range(inner // LANES):
        d = rate[:, tile(t)]
        a = jnp.exp(-d)
        strides[0, :, tile(t)] = jnp.exp(-float(CHUNK) * d)
        strides[1, :, tile(t)] = jnp.exp(-float(LANES) * d)
        power = a
        for j in range(CHUNK):
            powers[j * STATE : (j + 1) * STATE, tile(t)] = power.astype(bf16)
            power = power * a
        d = d * float(-2 * LANES)
        span = jnp.exp(d)
        own = span * keeps[0, 0:1, :]
        beside = span * keeps[1, 0:1, :]
        first_step[0, 0, :, tile(t)] = jnp.where(upper == 1, own, 1.0)
        first_step[0, 1, :, tile(t)] = jnp.where(upper == 1, 1.0, own)
        first_step[1, 0, :, tile(t)] = jnp.where(upper == 1, 1.0, beside)
        first_step[1, 1, :, tile(t)] = jnp.where(upper == 1, beside, 1.0)
        for m in range(1, keeps.shape[0] - 1):
            low, high, below = between(chip, m)
            lead = jnp.exp(d * (high - low).astype(f32)) * keeps[1 + m, 0:1, :]
            leads[m - 1, 0, :, tile(t)] = jnp.where(below, lead, 0.0)
            leads[m - 1, 1, :, tile(t)] = jnp.where(below, 0.0, lead)


def pair_kernel(ends, got, first_step, after_local, *sends):
    _, _, chip = spot()
    group = [
        (got[s].astype(f32) * first_step[0, s] + ends[s] * first_step[1, s]).astype(bf16)
        for s in range(STREAMS)
    ]
    for m, send in enumerate(sends):
        _, _, below = between(chip, m + 1)
        send[...] = jnp.where(below, group[1], group[0])


def columns(gated, w, out, part):
    inner, width = w.shape
    rows, half = out.shape
    base = pl.multiple_of(part * half, half)
    back = LANES - 1 - lax.broadcasted_iota(jnp.int32, (rows, LANES), 1)
    strip = min(BLOCK, half)
    for low in range(0, half, strip):
        here = pl.ds(pl.multiple_of(base + low, strip), strip)
        there = pl.ds(pl.multiple_of(width - base - low - strip, strip), strip)
        ahead = jnp.dot(gated[0], w[:, here], preferred_element_type=f32)
        behind = jnp.dot(gated[1], w[:, there], preferred_element_type=f32)
        for t in range(strip // LANES):
            turned = jnp.take_along_axis(behind[:, tile(strip // LANES - 1 - t)], back, axis=1)
            total = ahead[:, tile(t)] + turned
            out[:, low + t * LANES : low + (t + 1) * LANES] = total.astype(out.dtype)


def part_of(own):
    if lax.axis_size("ch") != 2:
        return jnp.int32(1 if own else 0)
    return lax.axis_index("ch") if own else 1 - lax.axis_index("ch")


def finish_kernel(
    same, powers, strides, got, leads, starts, y_f, y_b, readout_f, readout_b, z, w, *rest
):
    if same:
        *arrived, out, gated = rest
    else:
        *arrived, out, out_rest, gated = rest
    _, core, chip = spot()
    rows = out.shape[0]
    inner = w.shape[0]
    half = core if same else 1 - core
    base = pl.multiple_of(half * rows, rows)
    span = CHUNK * STATE
    local = (y_f, y_b)
    readouts = (readout_f, readout_b)
    for s in range(STREAMS):
        state = got[s].astype(f32) * jnp.where(chip & 1 == 1 - s, 1.0, 0.0)
        for m, part in enumerate(arrived):
            state = state + part[...].astype(f32) * leads[m, s]
        late = half == 1 - s
        state = state * jnp.where(late, strides[1], 1.0)
        first = jnp.where(late, rows // CHUNK, 0)
        for q in range(rows // CHUNK):
            row = q * CHUNK if s == 0 else rows - (q + 1) * CHUNK
            at = pl.ds(pl.multiple_of(base + row, CHUNK), CHUNK)
            begin = (state + starts[s, first + q]).astype(bf16)
            carried = powers[...].reshape(CHUNK, STATE, inner) * begin[None]
            state = state * strides[0]
            y = jnp.dot(
                readouts[s][at, :], carried.reshape(span, inner), preferred_element_type=f32
            )
            for t in range(inner // LANES):
                gated[s, row : row + CHUNK, tile(t)] = (
                    (y[:, tile(t)] + local[s][t, at, :])
                    * jax.nn.silu(z[s, at, tile(t)].astype(f32))
                ).astype(bf16)
    columns(gated, w, out, part_of(False))
    if not same:
        columns(gated, w, out_rest, part_of(True))


def rest_kernel(gated, w, after_first, out):
    columns(gated, w, out, part_of(True))


def body(
    hidden,
    tokens,
    edit_bounds,
    norm_gain,
    base_embed,
    w_in,
    conv_w,
    conv_b,
    proj_bc,
    decay_rate,
    skip_gain,
    w_out,
):
    rows = hidden.shape[0]
    width = w_in.shape[1]
    inner = w_in.shape[2] // 2
    tiles = inner // LANES
    length = 2 * rows
    padded = length + EDGE
    block = min(BLOCK, inner)
    seq_count = lax.axis_size("seq")
    ch_count = lax.axis_size("ch")
    chips = seq_count // 2
    chip = spot()[2]

    first, second = both_halves(hidden)
    rim = call(
        rim_kernel,
        "rim",
        shaped((EDGE, hidden.shape[1]), bf16),
        [ANYWHERE],
        [pltpu.SemaphoreType.DMA],
    )(in_hbm(hidden))
    later = pl.BlockSpec(memory_space=pl.ANY)
    rim_first, rim_second = rims(rim)
    channels = (STATE, inner)
    pairs = chips // 2
    (
        signal_w, gate_w, taps, offset, proj_half, rate, skip, gain, embed,
        bases, weigh, decay, keeps,
    ) = call(
        init_kernel,
        "init",
        [
            shaped((width, inner), bf16),
            shaped((width, inner), bf16),
            shaped((CONV, inner)),
            shaped((1, inner)),
            shaped((2 * STATE, inner), bf16),
            shaped(channels),
            shaped((1, inner)),
            shaped((1, width)),
            shaped((4, width)),
            shaped((rows + EDGE, LANES)),
            shaped((4 * 2 * STATE, rows)),
            shaped(channels),
            shaped((max(pairs, 1) + 1, SUBS, LANES)),
        ],
        [ANYWHERE] * 10 + [later],
        [
            pltpu.SMEM(edit_bounds.shape[::-1], jnp.int32),
            pltpu.VMEM((seq_count, rows), jnp.int32),
            pltpu.SemaphoreType.DMA((11,)),
        ],
    )(
        *(
            in_hbm(array)
            for array in (
                edit_bounds.T,
                tokens.reshape(seq_count, rows),
                w_in,
                conv_w,
                conv_b[None, :],
                proj_bc,
                decay_rate,
                skip_gain[None, :],
                norm_gain[None, :],
                base_embed,
            )
        ),
        rim,
    )
    drive = jnp.sqrt(-jnp.expm1(-2.0 * rate))
    normed = call(norm_kernel, "norm", shaped((rows + EDGE, width), bf16), [WHOLE] * 7)(
        first, second, rim_first, rim_second, bases, gain, embed
    )
    partner = swap(normed, "seq", 1)

    lined = shaped((2 * (rows + EDGE), width), bf16)
    lined_own, x_own = call(
        own_signal_kernel,
        "own_signal",
        [lined, shaped((2 * (rows + EDGE), inner))],
        [WHOLE] * 2,
    )(normed, signal_w)
    lined_other, c, bc = call(
        signal_kernel,
        "signal",
        [
            lined,
            shaped((STREAMS, tiles, length, LANES)),
            shaped((4 * 2 * STATE, rows)),
        ],
        [WHOLE] * 6,
        [pltpu.VMEM((2 * STREAMS * block // LANES, padded, LANES), f32)],
        megabytes=6,
    )(partner, x_own, signal_w, taps, offset, proj_half)
    bc = bc + swap(bc, "seq", 1)
    if ch_count == 2:
        bc_far = swap(bc, "ch", 1)
    else:
        bc, bc_far = lax.psum(bc, "ch"), jnp.zeros_like(bc)

    z = call(gate_kernel, "gate", shaped((STREAMS, length, inner), bf16), [WHOLE] * 3)(
        lined_own, lined_other, gate_w
    )
    scaled, ends, starts, out_w = call(
        end_kernel,
        "ends",
        [
            shaped((4 * 2 * STATE, rows)),
            shaped((STREAMS,) + channels),
            shaped((STREAMS, length // CHUNK) + channels),
            shaped((inner, width), bf16),
        ],
        [WHOLE] * 7 + [later, ANYWHERE],
        [pltpu.VMEM((STREAMS, length * STATE, LANES), f32), pltpu.SemaphoreType.DMA],
        megabytes=6,
    )(bc, bc_far, weigh, c, decay, drive, keeps, z, in_hbm(w_out))

    got = swap(ends.astype(bf16), "seq", 2)
    strides, powers, first_step, leads = call(
        factor_kernel,
        "factors",
        [
            shaped((2,) + channels),
            shaped((CHUNK * STATE, inner), bf16),
            shaped((2, STREAMS) + channels),
            shaped((max(pairs - 1, 1), STREAMS) + channels),
        ],
        [WHOLE] * 2 + [later],
    )(rate, keeps, scaled)
    by_tile = (tiles, length, LANES)

    def local(s, after):
        return call(
            functools.partial(local_kernel, s),
            "local",
            [shaped(by_tile), shaped((length, CHUNK * STATE), bf16)],
            [WHOLE] * 5 + [later],
            [
                pltpu.VMEM((2, length, LANES), f32),
                pltpu.VMEM(by_tile, f32),
                pltpu.VMEM(by_tile, f32),
            ],
            megabytes=6,
        )(scaled, c, decay, drive, skip, after)

    y_f, readout_f = local(0, ends)
    arrived = []
    if pairs > 1:
        sends = call(
            pair_kernel,
            "pairs",
            [shaped(channels, bf16)] * (pairs - 1),
            [WHOLE] * 3 + [later],
        )(ends, got, first_step, y_f)
        arrived = [swap(send, "seq", 4 * m) for m, send in enumerate(sends, 1)]
    y_b, readout_b = local(1, sends[0] if pairs > 1 else got)

    operands = (
        powers, strides, got, leads, starts, y_f, y_b, readout_f, readout_b, z, out_w, *arrived
    )
    half_width = (rows, width // 2)
    gated = (STREAMS, rows, inner)
    both = call(
        functools.partial(finish_kernel, False),
        "finish",
        [shaped(half_width, bf16)] * 2,
        [WHOLE] * len(operands),
        [pltpu.VMEM(gated, bf16)],
    )(*operands)
    first_far, second_far = [swap(send, "seq", 1) for send in both]
    first, gated_own = call(
        functools.partial(finish_kernel, True),
        "finish",
        [shaped(half_width), shaped(gated, bf16)],
        [WHOLE] * len(operands),
    )(*operands)
    first = first + first_far.astype(f32)
    sent = first.astype(bf16)
    if ch_count == 2:
        came = swap(sent, "ch", 1)
    second = call(rest_kernel, "rest", shaped(half_width), [WHOLE] * 2 + [later])(
        gated_own, out_w, sent
    )
    second = second + second_far.astype(f32)
    if ch_count == 2:
        return (second + came.astype(f32)).astype(bf16)
    total = jnp.concatenate([first, second], axis=1)
    return lax.psum_scatter(total.astype(bf16), "ch", scatter_dimension=1, tiled=True)


def solution(mesh):
    placed = (
        P("seq", "ch"),
        P(),
        P(),
        P(),
        P(),
        P(None, None, "ch"),
        P(None, "ch"),
        P("ch"),
        P(None, "ch"),
        P(None, "ch"),
        P("ch"),
        P("ch", None),
    )
    return jax.shard_map(
        body, mesh=mesh, in_specs=placed, out_specs=P("seq", "ch"), check_vma=False
    )
```

```python
import functools

import jax
import jax.numpy as jnp
from jax import lax
from jax.experimental import pallas as pl
from jax.experimental.pallas import tpu as pltpu
from jax.sharding import PartitionSpec as P

CONV = 4
STATE = 16
EDGE = 16
LANES = 128
SUBS = 8
STREAMS = 2
CHUNK = 16
BLOCK = 256
HALVES = 2
epsilon = 1e-05
f32 = jnp.float32
bf16 = jnp.bfloat16

WHOLE = pl.BlockSpec(memory_space=pltpu.VMEM)
SCALARS = pl.BlockSpec(memory_space=pltpu.SMEM)
ANYWHERE = pl.BlockSpec(memory_space=pltpu.HBM)


def shaped(shape, dtype=f32):
    return jax.ShapeDtypeStruct(shape, dtype)


def call(kernel, name, outs, ins, scratch=(), megabytes=4):
    return pl.pallas_call(
        kernel,
        out_shape=outs,
        in_specs=ins,
        out_specs=jax.tree.map(lambda _: WHOLE, outs),
        scratch_shapes=list(scratch),
        compiler_params=pltpu.CompilerParams(vmem_limit_bytes=megabytes << 20),
        name=name,
    )


def tile(t):
    return slice(t * LANES, (t + 1) * LANES)


def spot():
    place = lax.axis_index("seq")
    return place, place & 1, place >> 1


def swap(block, axis, apart):
    count = lax.axis_size(axis)
    return lax.ppermute(block, axis, [(i, i ^ apart) for i in range(count)])


def in_hbm(array):
    return pltpu.with_memory_space_constraint(array, pltpu.HBM)


def both_halves(block):
    if lax.axis_size("ch") == 2:
        return block, swap(block, "ch", 1)
    full = lax.all_gather(block, "ch", axis=1, tiled=True)
    half = full.shape[1] // 2
    return full[:, :half], full[:, half:]


def rims(rim):
    seq_count, ch_count = lax.axis_size("seq"), lax.axis_size("ch")
    pairs = [(i, i + 1) for i in range(1, seq_count - 1, 2)]
    pairs = pairs + [(j, i) for i, j in pairs]
    if ch_count != 2:
        return both_halves(lax.ppermute(rim, "seq", pairs))
    return tuple(
        lax.ppermute(
            rim,
            ("seq", "ch"),
            [(i * ch_count + (k ^ apart), j * ch_count + k) for i, j in pairs for k in range(2)],
        )
        for apart in range(2)
    )


def rim_kernel(hidden, rim, sem):
    low = pl.multiple_of(spot()[1] * (hidden.shape[0] - EDGE), EDGE)
    copy = pltpu.make_async_copy(hidden.at[pl.ds(low, EDGE), :], rim, sem)
    copy.start()
    copy.wait()


def between(chip, m):
    pair = chip >> 1
    other = pair ^ m
    below = other < pair
    return jnp.where(below, 2 * other + 2, chip + 1), jnp.where(below, chip, 2 * other), below


def init_kernel(
    bounds_all, tokens_all, w_in, conv_w, conv_b, proj, rate_all, skip, gain_all, embed_all, after,
    signal_w, gate_w, taps, offset, proj_half, rate, skip_half, norm_gain, embed,
    bases, weigh, decay, keeps, bounds, tokens, sems,
):
    place, core, chip = spot()
    count, rows = tokens.shape
    length = 2 * rows
    inner = rate.shape[1]
    chips = count // 2
    mine = pl.ds(pl.multiple_of(core * inner, inner), inner)
    copies = [
        pltpu.make_async_copy(source, target, sems.at[i])
        for i, (source, target) in enumerate(
            (
                (bounds_all, bounds),
                (rate_all.at[:, mine], rate),
                (tokens_all, tokens),
                (gain_all, norm_gain),
                (embed_all, embed),
                (conv_w.at[:, mine], taps),
                (conv_b.at[:, mine], offset),
                (proj.at[:, mine], proj_half),
                (skip.at[:, mine], skip_half),
                (w_in.at[0, :, mine], signal_w),
                (w_in.at[1, :, mine], gate_w),
            )
        )
    ]
    for copy in copies:
        copy.start()

    copies[0].wait()
    marks = [bounds[k, i] for i in range(bounds.shape[1]) for k in range(2)]
    factors = []
    for i, mark in enumerate(marks):
        total = jnp.int32(1)
        earlier = jnp.int32(0)
        for k, other in enumerate(marks):
            same = jnp.where(other == mark, 1, 0)
            total = total + same
            if k < i:
                earlier = earlier + same
        factors.append(jnp.where(earlier > 0, 1, total).astype(f32))

    start = chip * length
    at = lax.broadcasted_iota(jnp.int32, (SUBS, rows), 1) + start
    for half in range(HALVES):
        runs = [jnp.ones((SUBS, rows), f32) for _ in range(STREAMS)]
        for mark, factor in zip(marks, factors):
            here = at + half * rows
            runs[0] = runs[0] * jnp.where((here >= mark) & (mark >= start), factor, 1.0)
            runs[1] = runs[1] * jnp.where((here <= mark) & (mark < start + length), factor, 1.0)
        for s in range(STREAMS):
            first = 2 * STATE * (2 * half + s)
            for k in range(STATE // SUBS):
                weigh[first + k * SUBS : first + (k + 1) * SUBS, :] = runs[s]
                low = first + STATE + k * SUBS
                weigh[low : low + SUBS, :] = 1.0 / runs[s]

    def kept(low, high):
        total = jnp.ones((SUBS, LANES), f32)
        for mark, factor in zip(marks, factors):
            total = total * jnp.where(
                (mark >= low * length) & (mark < high * length), factor, 1.0
            )
        return 1.0 / total

    keeps[0] = kept(chip, chip + 1)
    keeps[1] = kept(chip ^ 1, (chip ^ 1) + 1)
    for m in range(1, chips // 2):
        low, high, _ = between(chip, m)
        keeps[1 + m] = kept(low, high)
    copies[1].wait()
    for t in range(inner // LANES):
        decay[:, tile(t)] = jnp.exp(-rate[:, tile(t)])

    copies[2].wait()

    def column(row):
        line = tokens[pl.ds(row, 1), :].astype(f32)
        return jnp.broadcast_to(line, (rows, rows)).T

    bases[:rows, :] = column(place)
    beyond = column(jnp.clip(jnp.where(core == 0, place - 1, place + 1), 0, count - 1))
    beyond = jnp.where(core == 0, beyond[rows - EDGE :], beyond[:EDGE])
    inside = jnp.where(core == 0, place > 0, place < count - 1)
    bases[rows:, :] = jnp.where(inside, beyond, -1.0)
    for copy in copies[3:]:
        copy.wait()


def norm_kernel(own, far, own_rim, far_rim, bases, gain, embed, out):
    rows = own.shape[0]
    half = own.shape[1]
    index = lax.axis_index("ch") if lax.axis_size("ch") == 2 else jnp.int32(0)

    def one(first, second, low, count):
        marks = bases[low : low + count, :]
        total = jnp.zeros((count, LANES), f32)
        for part in (first, second):
            for t in range(half // LANES):
                v = part[:, tile(t)].astype(f32)
                total = total + v * v
        inv_rms = lax.rsqrt(jnp.sum(total, axis=1, keepdims=True) / (2 * half) + epsilon)
        inv_rms = jnp.broadcast_to(inv_rms, (count, LANES))
        for k, part in enumerate((first, second)):
            for t in range(half // LANES):
                cols = slice(k * half + t * LANES, k * half + (t + 1) * LANES)
                e = [embed[b : b + 1, cols] for b in range(4)]
                added = jnp.where(
                    marks < 0.5, e[0], jnp.where(marks < 1.5, e[1], jnp.where(marks < 2.5, e[2], e[3]))
                )
                v = part[:, tile(t)].astype(f32) * inv_rms * gain[0:1, cols] + added
                out[low : low + count, cols] = jnp.where(marks < -0.5, 0.0, v).astype(bf16)

    @pl.when(index == 0)
    def _():
        one(own, far, 0, rows)
        one(own_rim, far_rim, rows, EDGE)

    @pl.when(index != 0)
    def _():
        one(far, own, 0, rows)
        one(far_rim, own_rim, rows, EDGE)


def both_ways(normed, lined):
    count, width = normed.shape
    lined[:count, :] = normed[...]
    r = lax.broadcasted_iota(jnp.int32, (LANES, LANES), 0)
    q = lax.broadcasted_iota(jnp.int32, (LANES, LANES), 1)
    turn = jnp.where(r + q == LANES - 1, 1.0, 0.0).astype(bf16)
    for t in range(width // LANES):
        piece = normed[:, tile(width // LANES - 1 - t)]
        lined[count:, tile(t)] = jnp.dot(piece, turn, preferred_element_type=f32).astype(bf16)


def own_signal_kernel(normed, w, lined, x_out):
    inner = w.shape[1]
    block = min(BLOCK, inner)
    both_ways(normed, lined)
    for b in range(inner // block):
        cols = slice(b * block, (b + 1) * block)
        x = jnp.dot(lined[...], w[:, cols], preferred_element_type=f32)
        x_out[:, cols] = x.astype(bf16).astype(f32)


def signal_kernel(
    normed, x_own, w, taps, offset, proj, lined, c_out, bc_out, x_tiles
):
    _, core, _ = spot()
    count = normed.shape[0]
    rows = count - EDGE
    length = 2 * rows
    inner = w.shape[1]
    block = min(BLOCK, inner)
    tiles = block // LANES
    both_ways(normed, lined)
    inner_bc = 2 * STATE
    sums = [jnp.zeros((inner_bc, rows), f32) for _ in range(STREAMS * HALVES)]

    def project(b):
        other = jnp.dot(
            lined[...], w[:, b * block : (b + 1) * block], preferred_element_type=f32
        )
        other = other.astype(bf16).astype(f32)
        for s in range(STREAMS):
            first = EDGE * (1 - s)
            low = s * count
            for t in range(tiles):
                slot = (b % 2 * STREAMS + s) * tiles + t
                mine = x_own[low : low + count, tile(b * tiles + t)]
                far = other[low : low + count, tile(t)]
                x_tiles[slot, first : first + rows, :] = jnp.where(
                    core == 0, mine[:rows], far[:rows]
                )
                x_tiles[slot, first + rows : first + length, :] = jnp.where(
                    core == 0, far[:rows], mine[:rows]
                )
                x_tiles[slot, s * length : s * length + EDGE, :] = jnp.where(
                    core == s, mine[rows:], far[rows:]
                )

    def convolve(b, s):
        mixed = []
        for t in range(tiles):
            slot = (b % 2 * STREAMS + s) * tiles + t
            cols = tile(b * tiles + t)
            total = offset[0:1, cols]
            for k in range(CONV):
                at = EDGE - CONV + 1 + k if s == 0 else CONV - 1 - k
                total = total + x_tiles[slot, at : at + length, :] * taps[k : k + 1, cols]
            c = jax.nn.silu(total).astype(bf16)
            c_out[s, b * tiles + t] = c.astype(f32)
            mixed.append(c)
        mixed = mixed[0] if tiles == 1 else jnp.concatenate(mixed, axis=1)
        for half in range(HALVES):
            sums[2 * half + s] = sums[2 * half + s] + lax.dot_general(
                proj[:, b * block : (b + 1) * block],
                mixed[half * rows : (half + 1) * rows],
                (((1,), (1,)), ((), ())),
                preferred_element_type=f32,
            )

    blocks = inner // block
    project(0)
    for b in range(blocks):
        if b + 1 < blocks:
            project(b + 1)
        for s in range(STREAMS):
            convolve(b, s)
    for i, total in enumerate(sums):
        bc_out[i * inner_bc : (i + 1) * inner_bc, :] = total


def gate_kernel(lined_own, lined_other, w, z_out):
    _, core, _ = spot()
    count = lined_own.shape[0] // 2
    rows = count - EDGE
    inner = w.shape[1]
    block = min(BLOCK, inner)
    for b in range(inner // block):
        cols = slice(b * block, (b + 1) * block)
        for lined, half in ((lined_own, core), (lined_other, 1 - core)):
            z = jnp.dot(lined[...], w[:, cols], preferred_element_type=f32).astype(bf16)
            at = pl.ds(pl.multiple_of(half * rows, rows), rows)
            for s in range(STREAMS):
                z_out[s, at, cols] = z[s * count : s * count + rows]


def lane_of(values, lane):
    return jnp.take_along_axis(values, jnp.full(values.shape, lane, jnp.int32), axis=1)


def tiles_of(ref, count):
    return [ref[h * SUBS : (h + 1) * SUBS, tile(t)] for t in range(count) for h in range(2)]


def spread(bc, wide):
    rows = bc.shape[1]
    across = STREAMS * LANES
    r = lax.broadcasted_iota(jnp.int32, (STREAMS * rows, across), 0)
    q = lax.broadcasted_iota(jnp.int32, (STREAMS * rows, across), 1)
    ones = jnp.where(r // rows == q // LANES, 1.0, 0.0).astype(bf16)
    lanes = lax.broadcasted_iota(jnp.int32, (STATE, STREAMS * rows), 1) & (rows - 1)
    group = 8
    for half in range(HALVES):
        firsts = [2 * STATE * (2 * half + s) for s in range(STREAMS)]
        entries = jnp.concatenate([bc[low : low + STATE, :] for low in firsts], axis=1)
        for j in range(0, rows, group):
            alone = jnp.concatenate(
                [jnp.where(lanes == j + i, entries, 0.0).astype(bf16) for i in range(group)], axis=0
            )
            at = (half * rows + j) * STATE
            found = jnp.dot(alone, ones, preferred_element_type=f32)
            for s in range(STREAMS):
                wide[s, at : at + group * STATE, :] = found[:, tile(s)]


def end_kernel(
    bc_own, bc_far, weigh, c, decay, drive, keeps, after_z, w,
    bc_out, end_out, starts, w_out, wide, sem,
):
    inner = w_out.shape[0]
    mine = pl.ds(pl.multiple_of(spot()[1] * inner, inner), inner)
    fetch = pltpu.make_async_copy(w.at[mine, :], w_out, sem)
    fetch.start()
    rows = bc_own.shape[1]
    length = 2 * rows
    count = c.shape[1]
    bc_out[...] = (bc_own[...] + bc_far[...]) * weigh[...]
    spread(bc_out, wide)
    a = tiles_of(decay, count)

    def chunk(n, state):
        for s in range(STREAMS):
            for t in range(count):
                for h in range(2):
                    sub = slice(h * SUBS, (h + 1) * SUBS)
                    starts[s, n, sub, tile(t)] = (
                        state[s * 2 * count + 2 * t + h] * drive[sub, tile(t)]
                    )
        for j in range(CHUNK):
            after = []
            for s in range(STREAMS):
                t0 = n * CHUNK + j if s == 0 else length - 1 - n * CHUNK - j
                low = pl.multiple_of(t0 * STATE, STATE)
                b = [wide[s, pl.ds(low + h * SUBS, SUBS), :] for h in range(2)]
                for t in range(count):
                    x = c[s, t, pl.ds(t0, 1), :]
                    for h in range(2):
                        i = 2 * t + h
                        after.append(a[i] * state[s * 2 * count + i] + b[h] * x)
            state = tuple(after)
        return state

    zero = jnp.zeros((SUBS, LANES), f32)
    state = lax.fori_loop(0, length // CHUNK, chunk, (zero,) * (STREAMS * 2 * count))
    for s in range(STREAMS):
        for t in range(count):
            for h in range(2):
                sub = slice(h * SUBS, (h + 1) * SUBS)
                end_out[s, sub, tile(t)] = (
                    state[s * 2 * count + 2 * t + h] * drive[sub, tile(t)] * keeps[0, 0:1, :]
                )
    fetch.wait()


def local_kernel(
    stream, bc, c, decay, drive, skip, after, y_out, readout, lined, c_lined, y_lined
):
    rows = bc.shape[1]
    length = 2 * rows
    count = c.shape[1]
    span = CHUNK * STATE
    places = length // CHUNK
    turned = bc[...].T
    r = lax.broadcasted_iota(jnp.int32, (rows, span), 0)
    q = lax.broadcasted_iota(jnp.int32, (rows, span), 1)
    step = r & (CHUNK - 1) if stream == 0 else CHUNK - 1 - (r & (CHUNK - 1))
    for half in range(HALVES):
        column = 2 * STATE * (2 * half + stream)
        pick = jnp.where(r == column + STATE + (q & (STATE - 1)), 1.0, 0.0).astype(bf16)
        picked = jnp.dot(turned.astype(bf16), pick, preferred_element_type=f32)
        readout[half * rows : (half + 1) * rows, :] = jnp.where(
            q // STATE == step, picked, 0.0
        ).astype(bf16)
        lined[0, half * rows : (half + 1) * rows, :] = (
            turned if column == 0 else pltpu.roll(turned, LANES - column, 1)
        )
    for j in range(CHUNK):
        to = slice(j * places, (j + 1) * places)
        lined[1, to, :] = lined[0, pl.ds(j, places, stride=CHUNK), :]
        for t in range(count):
            c_lined[t, to, :] = c[stream, t, pl.ds(j, places, stride=CHUNK), :]
    inputs = lined[1]
    outputs = pltpu.roll(inputs, LANES - STATE, 1)
    block = min(2, count)
    for low in range(0, count, block):
        wide = slice(low * LANES, (low + block) * LANES)
        reach = drive[:, wide]
        for lag in range(CHUNK):
            shift = lag * places
            near, far = slice(shift, length), slice(0, length - shift)
            if stream == 1:
                near, far = far, near
            left = (outputs[near] * inputs[far])[:, :STATE].astype(bf16)
            found = jnp.dot(left, reach.astype(bf16), preferred_element_type=f32)
            for t in range(block):
                part = found[:, tile(t)]
                if lag == 0:
                    part = part + skip[0:1, tile(low + t)]
                part = part * c_lined[low + t, far, :]
                if lag == 0:
                    y_lined[low + t, near, :] = part
                else:
                    y_lined[low + t, near, :] += part
            reach = reach * decay[:, wide]
    for j in range(CHUNK):
        at = slice(j * places, (j + 1) * places)
        for t in range(count):
            y_out[t, pl.ds(j, places, stride=CHUNK), :] = y_lined[t, at, :]


def factor_kernel(rate, keeps, after_ends, strides, powers, first_step, leads):
    _, _, chip = spot()
    inner = rate.shape[1]
    upper = chip & 1
    for t in range(inner // LANES):
        d = rate[:, tile(t)]
        a = jnp.exp(-d)
        strides[0, :, tile(t)] = jnp.exp(-float(CHUNK) * d)
        strides[1, :, tile(t)] = jnp.exp(-float(LANES) * d)
        power = a
        for j in range(CHUNK):
            powers[j * STATE : (j + 1) * STATE, tile(t)] = power.astype(bf16)
            power = power * a
        d = d * float(-2 * LANES)
        span = jnp.exp(d)
        own = span * keeps[0, 0:1, :]
        beside = span * keeps[1, 0:1, :]
        first_step[0, 0, :, tile(t)] = jnp.where(upper == 1, own, 1.0)
        first_step[0, 1, :, tile(t)] = jnp.where(upper == 1, 1.0, own)
        first_step[1, 0, :, tile(t)] = jnp.where(upper == 1, 1.0, beside)
        first_step[1, 1, :, tile(t)] = jnp.where(upper == 1, beside, 1.0)
        for m in range(1, keeps.shape[0] - 1):
            low, high, below = between(chip, m)
            lead = jnp.exp(d * (high - low).astype(f32)) * keeps[1 + m, 0:1, :]
            leads[m - 1, 0, :, tile(t)] = jnp.where(below, lead, 0.0)
            leads[m - 1, 1, :, tile(t)] = jnp.where(below, 0.0, lead)


def pair_kernel(ends, got, first_step, after_local, *sends):
    _, _, chip = spot()
    group = [
        (got[s].astype(f32) * first_step[0, s] + ends[s] * first_step[1, s]).astype(bf16)
        for s in range(STREAMS)
    ]
    for m, send in enumerate(sends):
        _, _, below = between(chip, m + 1)
        send[...] = jnp.where(below, group[1], group[0])


def columns(gated, w, out, part):
    inner, width = w.shape
    rows, half = out.shape
    base = pl.multiple_of(part * half, half)
    back = LANES - 1 - lax.broadcasted_iota(jnp.int32, (rows, LANES), 1)
    strip = min(BLOCK, half)
    for low in range(0, half, strip):
        here = pl.ds(pl.multiple_of(base + low, strip), strip)
        there = pl.ds(pl.multiple_of(width - base - low - strip, strip), strip)
        ahead = jnp.dot(gated[0], w[:, here], preferred_element_type=f32)
        behind = jnp.dot(gated[1], w[:, there], preferred_element_type=f32)
        for t in range(strip // LANES):
            turned = jnp.take_along_axis(behind[:, tile(strip // LANES - 1 - t)], back, axis=1)
            total = ahead[:, tile(t)] + turned
            out[:, low + t * LANES : low + (t + 1) * LANES] = total.astype(out.dtype)


def part_of(own):
    if lax.axis_size("ch") != 2:
        return jnp.int32(1 if own else 0)
    return lax.axis_index("ch") if own else 1 - lax.axis_index("ch")


def finish_kernel(
    same, powers, strides, got, leads, starts, y_f, y_b, readout_f, readout_b, z, w, *rest
):
    if same:
        *arrived, out, gated = rest
    else:
        *arrived, out, out_rest, gated = rest
    _, core, chip = spot()
    rows = out.shape[0]
    inner = w.shape[0]
    half = core if same else 1 - core
    base = pl.multiple_of(half * rows, rows)
    span = CHUNK * STATE
    local = (y_f, y_b)
    readouts = (readout_f, readout_b)
    for s in range(STREAMS):
        state = got[s].astype(f32) * jnp.where(chip & 1 == 1 - s, 1.0, 0.0)
        for m, part in enumerate(arrived):
            state = state + part[...].astype(f32) * leads[m, s]
        late = half == 1 - s
        state = state * jnp.where(late, strides[1], 1.0)
        first = jnp.where(late, rows // CHUNK, 0)
        for q in range(rows // CHUNK):
            row = q * CHUNK if s == 0 else rows - (q + 1) * CHUNK
            at = pl.ds(pl.multiple_of(base + row, CHUNK), CHUNK)
            begin = (state + starts[s, first + q]).astype(bf16)
            carried = powers[...].reshape(CHUNK, STATE, inner) * begin[None]
            state = state * strides[0]
            y = jnp.dot(
                readouts[s][at, :], carried.reshape(span, inner), preferred_element_type=f32
            )
            for t in range(inner // LANES):
                gated[s, row : row + CHUNK, tile(t)] = (
                    (y[:, tile(t)] + local[s][t, at, :])
                    * jax.nn.silu(z[s, at, tile(t)].astype(f32))
                ).astype(bf16)
    columns(gated, w, out, part_of(False))
    if not same:
        columns(gated, w, out_rest, part_of(True))


def rest_kernel(gated, w, after_first, out):
    columns(gated, w, out, part_of(True))


def body(
    hidden,
    tokens,
    edit_bounds,
    norm_gain,
    base_embed,
    w_in,
    conv_w,
    conv_b,
    proj_bc,
    decay_rate,
    skip_gain,
    w_out,
):
    rows = hidden.shape[0]
    width = w_in.shape[1]
    inner = w_in.shape[2] // 2
    tiles = inner // LANES
    length = 2 * rows
    padded = length + EDGE
    block = min(BLOCK, inner)
    seq_count = lax.axis_size("seq")
    ch_count = lax.axis_size("ch")
    chips = seq_count // 2
    chip = spot()[2]

    first, second = both_halves(hidden)
    rim = call(
        rim_kernel,
        "rim",
        shaped((EDGE, hidden.shape[1]), bf16),
        [ANYWHERE],
        [pltpu.SemaphoreType.DMA],
    )(in_hbm(hidden))
    later = pl.BlockSpec(memory_space=pl.ANY)
    rim_first, rim_second = rims(rim)
    channels = (STATE, inner)
    pairs = chips // 2
    (
        signal_w, gate_w, taps, offset, proj_half, rate, skip, gain, embed,
        bases, weigh, decay, keeps,
    ) = call(
        init_kernel,
        "init",
        [
            shaped((width, inner), bf16),
            shaped((width, inner), bf16),
            shaped((CONV, inner)),
            shaped((1, inner)),
            shaped((2 * STATE, inner), bf16),
            shaped(channels),
            shaped((1, inner)),
            shaped((1, width)),
            shaped((4, width)),
            shaped((rows + EDGE, LANES)),
            shaped((4 * 2 * STATE, rows)),
            shaped(channels),
            shaped((max(pairs, 1) + 1, SUBS, LANES)),
        ],
        [ANYWHERE] * 10 + [later],
        [
            pltpu.SMEM(edit_bounds.shape[::-1], jnp.int32),
            pltpu.VMEM((seq_count, rows), jnp.int32),
            pltpu.SemaphoreType.DMA((11,)),
        ],
    )(
        *(
            in_hbm(array)
            for array in (
                edit_bounds.T,
                tokens.reshape(seq_count, rows),
                w_in,
                conv_w,
                conv_b[None, :],
                proj_bc,
                decay_rate,
                skip_gain[None, :],
                norm_gain[None, :],
                base_embed,
            )
        ),
        rim,
    )
    drive = jnp.sqrt(-jnp.expm1(-2.0 * rate))
    normed = call(norm_kernel, "norm", shaped((rows + EDGE, width), bf16), [WHOLE] * 7)(
        first, second, rim_first, rim_second, bases, gain, embed
    )
    partner = swap(normed, "seq", 1)

    lined = shaped((2 * (rows + EDGE), width), bf16)
    lined_own, x_own = call(
        own_signal_kernel,
        "own_signal",
        [lined, shaped((2 * (rows + EDGE), inner))],
        [WHOLE] * 2,
    )(normed, signal_w)
    lined_other, c, bc = call(
        signal_kernel,
        "signal",
        [
            lined,
            shaped((STREAMS, tiles, length, LANES)),
            shaped((4 * 2 * STATE, rows)),
        ],
        [WHOLE] * 6,
        [pltpu.VMEM((2 * STREAMS * block // LANES, padded, LANES), f32)],
        megabytes=6,
    )(partner, x_own, signal_w, taps, offset, proj_half)
    bc = bc + swap(bc, "seq", 1)
    if ch_count == 2:
        bc_far = swap(bc, "ch", 1)
    else:
        bc, bc_far = lax.psum(bc, "ch"), jnp.zeros_like(bc)

    z = call(gate_kernel, "gate", shaped((STREAMS, length, inner), bf16), [WHOLE] * 3)(
        lined_own, lined_other, gate_w
    )
    scaled, ends, starts, out_w = call(
        end_kernel,
        "ends",
        [
            shaped((4 * 2 * STATE, rows)),
            shaped((STREAMS,) + channels),
            shaped((STREAMS, length // CHUNK) + channels),
            shaped((inner, width), bf16),
        ],
        [WHOLE] * 7 + [later, ANYWHERE],
        [pltpu.VMEM((STREAMS, length * STATE, LANES), f32), pltpu.SemaphoreType.DMA],
        megabytes=6,
    )(bc, bc_far, weigh, c, decay, drive, keeps, z, in_hbm(w_out))

    got = swap(ends.astype(bf16), "seq", 2)
    strides, powers, first_step, leads = call(
        factor_kernel,
        "factors",
        [
            shaped((2,) + channels),
            shaped((CHUNK * STATE, inner), bf16),
            shaped((2, STREAMS) + channels),
            shaped((max(pairs - 1, 1), STREAMS) + channels),
        ],
        [WHOLE] * 2 + [later],
    )(rate, keeps, scaled)
    by_tile = (tiles, length, LANES)

    def local(s, after):
        return call(
            functools.partial(local_kernel, s),
            "local",
            [shaped(by_tile), shaped((length, CHUNK * STATE), bf16)],
            [WHOLE] * 5 + [later],
            [
                pltpu.VMEM((2, length, LANES), f32),
                pltpu.VMEM(by_tile, f32),
                pltpu.VMEM(by_tile, f32),
            ],
            megabytes=6,
        )(scaled, c, decay, drive, skip, after)

    y_f, readout_f = local(0, ends)
    arrived = []
    if pairs > 1:
        sends = call(
            pair_kernel,
            "pairs",
            [shaped(channels, bf16)] * (pairs - 1),
            [WHOLE] * 3 + [later],
        )(ends, got, first_step, y_f)
        arrived = [swap(send, "seq", 4 * m) for m, send in enumerate(sends, 1)]
    y_b, readout_b = local(1, sends[0] if pairs > 1 else got)

    operands = (
        powers, strides, got, leads, starts, y_f, y_b, readout_f, readout_b, z, out_w, *arrived
    )
    half_width = (rows, width // 2)
    gated = (STREAMS, rows, inner)
    both = call(
        functools.partial(finish_kernel, False),
        "finish",
        [shaped(half_width, bf16)] * 2,
        [WHOLE] * len(operands),
        [pltpu.VMEM(gated, bf16)],
    )(*operands)
    first_far, second_far = [swap(send, "seq", 1) for send in both]
    first, gated_own = call(
        functools.partial(finish_kernel, True),
        "finish",
        [shaped(half_width), shaped(gated, bf16)],
        [WHOLE] * len(operands),
    )(*operands)
    first = first + first_far.astype(f32)
    sent = first.astype(bf16)
    if ch_count == 2:
        came = swap(sent, "ch", 1)
    second = call(rest_kernel, "rest", shaped(half_width), [WHOLE] * 2 + [later])(
        gated_own, out_w, sent
    )
    second = second + second_far.astype(f32)
    if ch_count == 2:
        return (second + came.astype(f32)).astype(bf16)
    total = jnp.concatenate([first, second], axis=1)
    return lax.psum_scatter(total.astype(bf16), "ch", scatter_dimension=1, tiled=True)


def solution(mesh):
    placed = (
        P("seq", "ch"),
        P(),
        P(),
        P(),
        P(),
        P(None, None, "ch"),
        P(None, "ch"),
        P("ch"),
        P(None, "ch"),
        P(None, "ch"),
        P("ch"),
        P("ch", None),
    )
    return jax.shard_map(
        body, mesh=mesh, in_specs=placed, out_specs=P("seq", "ch"), check_vma=False
    )
```

```python
import functools

import jax
import jax.numpy as jnp
from jax import lax
from jax.experimental import pallas as pl
from jax.experimental.pallas import tpu as pltpu
from jax.sharding import PartitionSpec as P

CONV = 4
STATE = 16
EDGE = 16
LANES = 128
SUBS = 8
STREAMS = 2
CHUNK = 16
BLOCK = 256
HALVES = 2
epsilon = 1e-05
f32 = jnp.float32
bf16 = jnp.bfloat16

WHOLE = pl.BlockSpec(memory_space=pltpu.VMEM)
SCALARS = pl.BlockSpec(memory_space=pltpu.SMEM)
ANYWHERE = pl.BlockSpec(memory_space=pltpu.HBM)


def shaped(shape, dtype=f32):
    return jax.ShapeDtypeStruct(shape, dtype)


def call(kernel, name, outs, ins, scratch=(), megabytes=4):
    return pl.pallas_call(
        kernel,
        out_shape=outs,
        in_specs=ins,
        out_specs=jax.tree.map(lambda _: WHOLE, outs),
        scratch_shapes=list(scratch),
        compiler_params=pltpu.CompilerParams(vmem_limit_bytes=megabytes << 20),
        name=name,
    )


def tile(t):
    return slice(t * LANES, (t + 1) * LANES)


def spot():
    place = lax.axis_index("seq")
    return place, place & 1, place >> 1


def swap(block, axis, apart):
    count = lax.axis_size(axis)
    return lax.ppermute(block, axis, [(i, i ^ apart) for i in range(count)])


def in_hbm(array):
    return pltpu.with_memory_space_constraint(array, pltpu.HBM)


def both_halves(block):
    if lax.axis_size("ch") == 2:
        return block, swap(block, "ch", 1)
    full = lax.all_gather(block, "ch", axis=1, tiled=True)
    half = full.shape[1] // 2
    return full[:, :half], full[:, half:]


def rims(rim):
    seq_count, ch_count = lax.axis_size("seq"), lax.axis_size("ch")
    pairs = [(i, i + 1) for i in range(1, seq_count - 1, 2)]
    pairs = pairs + [(j, i) for i, j in pairs]
    if ch_count != 2:
        return both_halves(lax.ppermute(rim, "seq", pairs))
    return tuple(
        lax.ppermute(
            rim,
            ("seq", "ch"),
            [(i * ch_count + (k ^ apart), j * ch_count + k) for i, j in pairs for k in range(2)],
        )
        for apart in range(2)
    )


def rim_kernel(hidden, rim, sem):
    low = pl.multiple_of(spot()[1] * (hidden.shape[0] - EDGE), EDGE)
    copy = pltpu.make_async_copy(hidden.at[pl.ds(low, EDGE), :], rim, sem)
    copy.start()
    copy.wait()


def between(chip, m):
    pair = chip >> 1
    other = pair ^ m
    below = other < pair
    return jnp.where(below, 2 * other + 2, chip + 1), jnp.where(below, chip, 2 * other), below


def init_kernel(
    bounds_all, tokens_all, w_in, conv_w, conv_b, proj, rate_all, skip, gain_all, embed_all, after,
    signal_w, gate_w, taps, offset, proj_half, rate, skip_half, norm_gain, embed,
    bases, weigh, decay, keeps, bounds, tokens, sems,
):
    place, core, chip = spot()
    count, rows = tokens.shape
    length = 2 * rows
    inner = rate.shape[1]
    chips = count // 2
    mine = pl.ds(pl.multiple_of(core * inner, inner), inner)
    copies = [
        pltpu.make_async_copy(source, target, sems.at[i])
        for i, (source, target) in enumerate(
            (
                (bounds_all, bounds),
                (rate_all.at[:, mine], rate),
                (tokens_all, tokens),
                (gain_all, norm_gain),
                (embed_all, embed),
                (conv_w.at[:, mine], taps),
                (conv_b.at[:, mine], offset),
                (proj.at[:, mine], proj_half),
                (skip.at[:, mine], skip_half),
                (w_in.at[0, :, mine], signal_w),
                (w_in.at[1, :, mine], gate_w),
            )
        )
    ]
    for copy in copies:
        copy.start()

    copies[0].wait()
    marks = [bounds[k, i] for i in range(bounds.shape[1]) for k in range(2)]
    factors = []
    for i, mark in enumerate(marks):
        total = jnp.int32(1)
        earlier = jnp.int32(0)
        for k, other in enumerate(marks):
            same = jnp.where(other == mark, 1, 0)
            total = total + same
            if k < i:
                earlier = earlier + same
        factors.append(jnp.where(earlier > 0, 1, total).astype(f32))

    start = chip * length
    at = lax.broadcasted_iota(jnp.int32, (SUBS, rows), 1) + start
    for half in range(HALVES):
        runs = [jnp.ones((SUBS, rows), f32) for _ in range(STREAMS)]
        for mark, factor in zip(marks, factors):
            here = at + half * rows
            runs[0] = runs[0] * jnp.where((here >= mark) & (mark >= start), factor, 1.0)
            runs[1] = runs[1] * jnp.where((here <= mark) & (mark < start + length), factor, 1.0)
        for s in range(STREAMS):
            first = 2 * STATE * (2 * half + s)
            for k in range(STATE // SUBS):
                weigh[first + k * SUBS : first + (k + 1) * SUBS, :] = runs[s]
                low = first + STATE + k * SUBS
                weigh[low : low + SUBS, :] = 1.0 / runs[s]

    def kept(low, high):
        total = jnp.ones((SUBS, LANES), f32)
        for mark, factor in zip(marks, factors):
            total = total * jnp.where(
                (mark >= low * length) & (mark < high * length), factor, 1.0
            )
        return 1.0 / total

    keeps[0] = kept(chip, chip + 1)
    keeps[1] = kept(chip ^ 1, (chip ^ 1) + 1)
    for m in range(1, chips // 2):
        low, high, _ = between(chip, m)
        keeps[1 + m] = kept(low, high)
    copies[1].wait()
    for t in range(inner // LANES):
        decay[:, tile(t)] = jnp.exp(-rate[:, tile(t)])

    copies[2].wait()

    def column(row):
        line = tokens[pl.ds(row, 1), :].astype(f32)
        return jnp.broadcast_to(line, (rows, rows)).T

    bases[:rows, :] = column(place)
    beyond = column(jnp.clip(jnp.where(core == 0, place - 1, place + 1), 0, count - 1))
    beyond = jnp.where(core == 0, beyond[rows - EDGE :], beyond[:EDGE])
    inside = jnp.where(core == 0, place > 0, place < count - 1)
    bases[rows:, :] = jnp.where(inside, beyond, -1.0)
    for copy in copies[3:]:
        copy.wait()


def norm_kernel(own, far, own_rim, far_rim, bases, gain, embed, out):
    rows = own.shape[0]
    half = own.shape[1]
    index = lax.axis_index("ch") if lax.axis_size("ch") == 2 else jnp.int32(0)

    def one(first, second, low, count):
        marks = bases[low : low + count, :]
        total = jnp.zeros((count, LANES), f32)
        for part in (first, second):
            for t in range(half // LANES):
                v = part[:, tile(t)].astype(f32)
                total = total + v * v
        inv_rms = lax.rsqrt(jnp.sum(total, axis=1, keepdims=True) / (2 * half) + epsilon)
        inv_rms = jnp.broadcast_to(inv_rms, (count, LANES))
        for k, part in enumerate((first, second)):
            for t in range(half // LANES):
                cols = slice(k * half + t * LANES, k * half + (t + 1) * LANES)
                e = [embed[b : b + 1, cols] for b in range(4)]
                added = jnp.where(
                    marks < 0.5, e[0], jnp.where(marks < 1.5, e[1], jnp.where(marks < 2.5, e[2], e[3]))
                )
                v = part[:, tile(t)].astype(f32) * inv_rms * gain[0:1, cols] + added
                out[low : low + count, cols] = jnp.where(marks < -0.5, 0.0, v).astype(bf16)

    @pl.when(index == 0)
    def _():
        one(own, far, 0, rows)
        one(own_rim, far_rim, rows, EDGE)

    @pl.when(index != 0)
    def _():
        one(far, own, 0, rows)
        one(far_rim, own_rim, rows, EDGE)


def both_ways(normed, lined):
    count, width = normed.shape
    lined[:count, :] = normed[...]
    r = lax.broadcasted_iota(jnp.int32, (LANES, LANES), 0)
    q = lax.broadcasted_iota(jnp.int32, (LANES, LANES), 1)
    turn = jnp.where(r + q == LANES - 1, 1.0, 0.0).astype(bf16)
    for t in range(width // LANES):
        piece = normed[:, tile(width // LANES - 1 - t)]
        lined[count:, tile(t)] = jnp.dot(piece, turn, preferred_element_type=f32).astype(bf16)


def own_signal_kernel(normed, w, lined, x_out):
    inner = w.shape[1]
    block = min(BLOCK, inner)
    both_ways(normed, lined)
    for b in range(inner // block):
        cols = slice(b * block, (b + 1) * block)
        x = jnp.dot(lined[...], w[:, cols], preferred_element_type=f32)
        x_out[:, cols] = x.astype(bf16).astype(f32)


def signal_kernel(
    normed, x_own, w, taps, offset, proj, lined, c_out, bc_out, x_tiles
):
    _, core, _ = spot()
    count = normed.shape[0]
    rows = count - EDGE
    length = 2 * rows
    inner = w.shape[1]
    block = min(BLOCK, inner)
    tiles = block // LANES
    both_ways(normed, lined)
    inner_bc = 2 * STATE
    sums = [jnp.zeros((inner_bc, rows), f32) for _ in range(STREAMS * HALVES)]

    def project(b):
        other = jnp.dot(
            lined[...], w[:, b * block : (b + 1) * block], preferred_element_type=f32
        )
        other = other.astype(bf16).astype(f32)
        for s in range(STREAMS):
            first = EDGE * (1 - s)
            low = s * count
            for t in range(tiles):
                slot = (b % 2 * STREAMS + s) * tiles + t
                mine = x_own[low : low + count, tile(b * tiles + t)]
                far = other[low : low + count, tile(t)]
                x_tiles[slot, first : first + rows, :] = jnp.where(
                    core == 0, mine[:rows], far[:rows]
                )
                x_tiles[slot, first + rows : first + length, :] = jnp.where(
                    core == 0, far[:rows], mine[:rows]
                )
                x_tiles[slot, s * length : s * length + EDGE, :] = jnp.where(
                    core == s, mine[rows:], far[rows:]
                )

    def convolve(b, s):
        mixed = []
        for t in range(tiles):
            slot = (b % 2 * STREAMS + s) * tiles + t
            cols = tile(b * tiles + t)
            total = offset[0:1, cols]
            for k in range(CONV):
                at = EDGE - CONV + 1 + k if s == 0 else CONV - 1 - k
                total = total + x_tiles[slot, at : at + length, :] * taps[k : k + 1, cols]
            c = jax.nn.silu(total).astype(bf16)
            c_out[s, b * tiles + t] = c.astype(f32)
            mixed.append(c)
        mixed = mixed[0] if tiles == 1 else jnp.concatenate(mixed, axis=1)
        for half in range(HALVES):
            sums[2 * half + s] = sums[2 * half + s] + lax.dot_general(
                proj[:, b * block : (b + 1) * block],
                mixed[half * rows : (half + 1) * rows],
                (((1,), (1,)), ((), ())),
                preferred_element_type=f32,
            )

    blocks = inner // block
    project(0)
    for b in range(blocks):
        if b + 1 < blocks:
            project(b + 1)
        for s in range(STREAMS):
            convolve(b, s)
    for i, total in enumerate(sums):
        bc_out[i * inner_bc : (i + 1) * inner_bc, :] = total


def gate_kernel(lined_own, lined_other, w, z_out):
    _, core, _ = spot()
    count = lined_own.shape[0] // 2
    rows = count - EDGE
    inner = w.shape[1]
    block = min(BLOCK, inner)
    for b in range(inner // block):
        cols = slice(b * block, (b + 1) * block)
        for lined, half in ((lined_own, core), (lined_other, 1 - core)):
            z = jnp.dot(lined[...], w[:, cols], preferred_element_type=f32).astype(bf16)
            at = pl.ds(pl.multiple_of(half * rows, rows), rows)
            for s in range(STREAMS):
                z_out[s, at, cols] = z[s * count : s * count + rows]


def lane_of(values, lane):
    return jnp.take_along_axis(values, jnp.full(values.shape, lane, jnp.int32), axis=1)


def tiles_of(ref, count):
    return [ref[h * SUBS : (h + 1) * SUBS, tile(t)] for t in range(count) for h in range(2)]


def spread(bc, wide, stream):
    rows = bc.shape[1]
    ones = jnp.ones((rows, LANES), bf16)
    lanes = lax.broadcasted_iota(jnp.int32, (STATE, rows), 1)
    group = 8
    for half in range(HALVES):
        first = 2 * STATE * (2 * half + stream)
        entries = bc[first : first + STATE, :]
        for j in range(0, rows, group):
            alone = jnp.concatenate(
                [jnp.where(lanes == j + i, entries, 0.0).astype(bf16) for i in range(group)], axis=0
            )
            at = (half * rows + j) * STATE
            wide[stream, at : at + group * STATE, :] = jnp.dot(
                alone, ones, preferred_element_type=f32
            )


def end_kernel(
    bc_own, bc_far, weigh, c, decay, drive, keeps, after_z, w,
    bc_out, end_out, starts, w_out, wide, sem,
):
    inner = w_out.shape[0]
    mine = pl.ds(pl.multiple_of(spot()[1] * inner, inner), inner)
    fetch = pltpu.make_async_copy(w.at[mine, :], w_out, sem)
    fetch.start()
    rows = bc_own.shape[1]
    length = 2 * rows
    count = c.shape[1]
    bc_out[...] = (bc_own[...] + bc_far[...]) * weigh[...]
    for s in range(STREAMS):
        spread(bc_out, wide, s)
    a = tiles_of(decay, count)

    def chunk(n, state):
        for s in range(STREAMS):
            for t in range(count):
                for h in range(2):
                    sub = slice(h * SUBS, (h + 1) * SUBS)
                    starts[s, n, sub, tile(t)] = (
                        state[s * 2 * count + 2 * t + h] * drive[sub, tile(t)]
                    )
        for j in range(CHUNK):
            after = []
            for s in range(STREAMS):
                t0 = n * CHUNK + j if s == 0 else length - 1 - n * CHUNK - j
                low = pl.multiple_of(t0 * STATE, STATE)
                b = [wide[s, pl.ds(low + h * SUBS, SUBS), :] for h in range(2)]
                for t in range(count):
                    x = c[s, t, pl.ds(t0, 1), :]
                    for h in range(2):
                        i = 2 * t + h
                        after.append(a[i] * state[s * 2 * count + i] + b[h] * x)
            state = tuple(after)
        return state

    zero = jnp.zeros((SUBS, LANES), f32)
    state = lax.fori_loop(0, length // CHUNK, chunk, (zero,) * (STREAMS * 2 * count))
    for s in range(STREAMS):
        for t in range(count):
            for h in range(2):
                sub = slice(h * SUBS, (h + 1) * SUBS)
                end_out[s, sub, tile(t)] = (
                    state[s * 2 * count + 2 * t + h] * drive[sub, tile(t)] * keeps[0, 0:1, :]
                )
    fetch.wait()


def local_kernel(
    stream, bc, c, decay, drive, skip, after, y_out, readout, lined, c_lined, y_lined
):
    rows = bc.shape[1]
    length = 2 * rows
    count = c.shape[1]
    span = CHUNK * STATE
    places = length // CHUNK
    turned = bc[...].T
    r = lax.broadcasted_iota(jnp.int32, (rows, span), 0)
    q = lax.broadcasted_iota(jnp.int32, (rows, span), 1)
    step = r & (CHUNK - 1) if stream == 0 else CHUNK - 1 - (r & (CHUNK - 1))
    for half in range(HALVES):
        column = 2 * STATE * (2 * half + stream)
        pick = jnp.where(r == column + STATE + (q & (STATE - 1)), 1.0, 0.0).astype(bf16)
        picked = jnp.dot(turned.astype(bf16), pick, preferred_element_type=f32)
        readout[half * rows : (half + 1) * rows, :] = jnp.where(
            q // STATE == step, picked, 0.0
        ).astype(bf16)
        lined[0, half * rows : (half + 1) * rows, :] = (
            turned if column == 0 else pltpu.roll(turned, LANES - column, 1)
        )
    for j in range(CHUNK):
        to = slice(j * places, (j + 1) * places)
        lined[1, to, :] = lined[0, pl.ds(j, places, stride=CHUNK), :]
        for t in range(count):
            c_lined[t, to, :] = c[stream, t, pl.ds(j, places, stride=CHUNK), :]
    inputs = lined[1]
    outputs = pltpu.roll(inputs, LANES - STATE, 1)
    block = min(2, count)
    for low in range(0, count, block):
        wide = slice(low * LANES, (low + block) * LANES)
        reach = drive[:, wide]
        for lag in range(CHUNK):
            shift = lag * places
            near, far = slice(shift, length), slice(0, length - shift)
            if stream == 1:
                near, far = far, near
            left = (outputs[near] * inputs[far])[:, :STATE].astype(bf16)
            found = jnp.dot(left, reach.astype(bf16), preferred_element_type=f32)
            for t in range(block):
                part = found[:, tile(t)]
                if lag == 0:
                    part = part + skip[0:1, tile(low + t)]
                part = part * c_lined[low + t, far, :]
                if lag == 0:
                    y_lined[low + t, near, :] = part
                else:
                    y_lined[low + t, near, :] += part
            reach = reach * decay[:, wide]
    for j in range(CHUNK):
        at = slice(j * places, (j + 1) * places)
        for t in range(count):
            y_out[t, pl.ds(j, places, stride=CHUNK), :] = y_lined[t, at, :]


def factor_kernel(rate, keeps, after_ends, strides, powers, first_step, leads):
    _, _, chip = spot()
    inner = rate.shape[1]
    upper = chip & 1
    for t in range(inner // LANES):
        d = rate[:, tile(t)]
        a = jnp.exp(-d)
        strides[0, :, tile(t)] = jnp.exp(-float(CHUNK) * d)
        strides[1, :, tile(t)] = jnp.exp(-float(LANES) * d)
        power = a
        for j in range(CHUNK):
            powers[j * STATE : (j + 1) * STATE, tile(t)] = power.astype(bf16)
            power = power * a
        d = d * float(-2 * LANES)
        span = jnp.exp(d)
        own = span * keeps[0, 0:1, :]
        beside = span * keeps[1, 0:1, :]
        first_step[0, 0, :, tile(t)] = jnp.where(upper == 1, own, 1.0)
        first_step[0, 1, :, tile(t)] = jnp.where(upper == 1, 1.0, own)
        first_step[1, 0, :, tile(t)] = jnp.where(upper == 1, 1.0, beside)
        first_step[1, 1, :, tile(t)] = jnp.where(upper == 1, beside, 1.0)
        for m in range(1, keeps.shape[0] - 1):
            low, high, below = between(chip, m)
            lead = jnp.exp(d * (high - low).astype(f32)) * keeps[1 + m, 0:1, :]
            leads[m - 1, 0, :, tile(t)] = jnp.where(below, lead, 0.0)
            leads[m - 1, 1, :, tile(t)] = jnp.where(below, 0.0, lead)


def pair_kernel(ends, got, first_step, after_local, *sends):
    _, _, chip = spot()
    group = [
        (got[s].astype(f32) * first_step[0, s] + ends[s] * first_step[1, s]).astype(bf16)
        for s in range(STREAMS)
    ]
    for k, send in enumerate(sends):
        _, _, below = between(chip, len(sends) - k)
        send[...] = jnp.where(below, group[1], group[0])


def columns(gated, w, out, part):
    inner, width = w.shape
    rows, half = out.shape
    base = pl.multiple_of(part * half, half)
    back = LANES - 1 - lax.broadcasted_iota(jnp.int32, (rows, LANES), 1)
    strip = min(BLOCK, half)
    for low in range(0, half, strip):
        here = pl.ds(pl.multiple_of(base + low, strip), strip)
        there = pl.ds(pl.multiple_of(width - base - low - strip, strip), strip)
        ahead = jnp.dot(gated[0], w[:, here], preferred_element_type=f32)
        behind = jnp.dot(gated[1], w[:, there], preferred_element_type=f32)
        for t in range(strip // LANES):
            turned = jnp.take_along_axis(behind[:, tile(strip // LANES - 1 - t)], back, axis=1)
            total = ahead[:, tile(t)] + turned
            out[:, low + t * LANES : low + (t + 1) * LANES] = total.astype(out.dtype)


def part_of(own):
    if lax.axis_size("ch") != 2:
        return jnp.int32(1 if own else 0)
    return lax.axis_index("ch") if own else 1 - lax.axis_index("ch")


def finish_kernel(
    same, powers, strides, got, leads, starts, y_f, y_b, readout_f, readout_b, z, w, *rest
):
    if same:
        *arrived, out, gated = rest
    else:
        *arrived, out, out_rest, gated = rest
    _, core, chip = spot()
    rows = out.shape[0]
    inner = w.shape[0]
    half = core if same else 1 - core
    base = pl.multiple_of(half * rows, rows)
    span = CHUNK * STATE
    local = (y_f, y_b)
    readouts = (readout_f, readout_b)
    for s in range(STREAMS):
        state = got[s].astype(f32) * jnp.where(chip & 1 == 1 - s, 1.0, 0.0)
        for m, part in enumerate(arrived):
            state = state + part[...].astype(f32) * leads[m, s]
        late = half == 1 - s
        state = state * jnp.where(late, strides[1], 1.0)
        first = jnp.where(late, rows // CHUNK, 0)
        for q in range(rows // CHUNK):
            row = q * CHUNK if s == 0 else rows - (q + 1) * CHUNK
            at = pl.ds(pl.multiple_of(base + row, CHUNK), CHUNK)
            begin = (state + starts[s, first + q]).astype(bf16)
            carried = powers[...].reshape(CHUNK, STATE, inner) * begin[None]
            state = state * strides[0]
            y = jnp.dot(
                readouts[s][at, :], carried.reshape(span, inner), preferred_element_type=f32
            )
            for t in range(inner // LANES):
                gated[s, row : row + CHUNK, tile(t)] = (
                    (y[:, tile(t)] + local[s][t, at, :])
                    * jax.nn.silu(z[s, at, tile(t)].astype(f32))
                ).astype(bf16)
    columns(gated, w, out, part_of(False))
    if not same:
        columns(gated, w, out_rest, part_of(True))


def rest_kernel(gated, w, after_first, out):
    columns(gated, w, out, part_of(True))


def body(
    hidden,
    tokens,
    edit_bounds,
    norm_gain,
    base_embed,
    w_in,
    conv_w,
    conv_b,
    proj_bc,
    decay_rate,
    skip_gain,
    w_out,
):
    rows = hidden.shape[0]
    width = w_in.shape[1]
    inner = w_in.shape[2] // 2
    tiles = inner // LANES
    length = 2 * rows
    padded = length + EDGE
    block = min(BLOCK, inner)
    seq_count = lax.axis_size("seq")
    ch_count = lax.axis_size("ch")
    chips = seq_count // 2
    chip = spot()[2]

    first, second = both_halves(hidden)
    rim = call(
        rim_kernel,
        "rim",
        shaped((EDGE, hidden.shape[1]), bf16),
        [ANYWHERE],
        [pltpu.SemaphoreType.DMA],
    )(in_hbm(hidden))
    later = pl.BlockSpec(memory_space=pl.ANY)
    rim_first, rim_second = rims(rim)
    channels = (STATE, inner)
    pairs = chips // 2
    (
        signal_w, gate_w, taps, offset, proj_half, rate, skip, gain, embed,
        bases, weigh, decay, keeps,
    ) = call(
        init_kernel,
        "init",
        [
            shaped((width, inner), bf16),
            shaped((width, inner), bf16),
            shaped((CONV, inner)),
            shaped((1, inner)),
            shaped((2 * STATE, inner), bf16),
            shaped(channels),
            shaped((1, inner)),
            shaped((1, width)),
            shaped((4, width)),
            shaped((rows + EDGE, LANES)),
            shaped((4 * 2 * STATE, rows)),
            shaped(channels),
            shaped((max(pairs, 1) + 1, SUBS, LANES)),
        ],
        [ANYWHERE] * 10 + [later],
        [
            pltpu.SMEM(edit_bounds.shape[::-1], jnp.int32),
            pltpu.VMEM((seq_count, rows), jnp.int32),
            pltpu.SemaphoreType.DMA((11,)),
        ],
    )(
        *(
            in_hbm(array)
            for array in (
                edit_bounds.T,
                tokens.reshape(seq_count, rows),
                w_in,
                conv_w,
                conv_b[None, :],
                proj_bc,
                decay_rate,
                skip_gain[None, :],
                norm_gain[None, :],
                base_embed,
            )
        ),
        rim,
    )
    drive = jnp.sqrt(-jnp.expm1(-2.0 * rate))
    normed = call(norm_kernel, "norm", shaped((rows + EDGE, width), bf16), [WHOLE] * 7)(
        first, second, rim_first, rim_second, bases, gain, embed
    )
    partner = swap(normed, "seq", 1)

    lined = shaped((2 * (rows + EDGE), width), bf16)
    lined_own, x_own = call(
        own_signal_kernel,
        "own_signal",
        [lined, shaped((2 * (rows + EDGE), inner))],
        [WHOLE] * 2,
    )(normed, signal_w)
    lined_other, c, bc = call(
        signal_kernel,
        "signal",
        [
            lined,
            shaped((STREAMS, tiles, length, LANES)),
            shaped((4 * 2 * STATE, rows)),
        ],
        [WHOLE] * 6,
        [pltpu.VMEM((2 * STREAMS * block // LANES, padded, LANES), f32)],
        megabytes=6,
    )(partner, x_own, signal_w, taps, offset, proj_half)
    bc = bc + swap(bc, "seq", 1)
    if ch_count == 2:
        bc_far = swap(bc, "ch", 1)
    else:
        bc, bc_far = lax.psum(bc, "ch"), jnp.zeros_like(bc)

    z = call(gate_kernel, "gate", shaped((STREAMS, length, inner), bf16), [WHOLE] * 3)(
        lined_own, lined_other, gate_w
    )
    scaled, ends, starts, out_w = call(
        end_kernel,
        "ends",
        [
            shaped((4 * 2 * STATE, rows)),
            shaped((STREAMS,) + channels),
            shaped((STREAMS, length // CHUNK) + channels),
            shaped((inner, width), bf16),
        ],
        [WHOLE] * 7 + [later, ANYWHERE],
        [pltpu.VMEM((STREAMS, length * STATE, LANES), f32), pltpu.SemaphoreType.DMA],
        megabytes=6,
    )(bc, bc_far, weigh, c, decay, drive, keeps, z, in_hbm(w_out))

    got = swap(ends.astype(bf16), "seq", 2)
    strides, powers, first_step, leads = call(
        factor_kernel,
        "factors",
        [
            shaped((2,) + channels),
            shaped((CHUNK * STATE, inner), bf16),
            shaped((2, STREAMS) + channels),
            shaped((max(pairs - 1, 1), STREAMS) + channels),
        ],
        [WHOLE] * 2 + [later],
    )(rate, keeps, scaled)
    by_tile = (tiles, length, LANES)

    def local(s, after):
        return call(
            functools.partial(local_kernel, s),
            "local",
            [shaped(by_tile), shaped((length, CHUNK * STATE), bf16)],
            [WHOLE] * 5 + [later],
            [
                pltpu.VMEM((2, length, LANES), f32),
                pltpu.VMEM(by_tile, f32),
                pltpu.VMEM(by_tile, f32),
            ],
            megabytes=6,
        )(scaled, c, decay, drive, skip, after)

    y_f, readout_f = local(0, ends)
    arrived = []
    if pairs > 1:
        sends = call(
            pair_kernel,
            "pairs",
            [shaped(channels, bf16)] * (pairs - 1),
            [WHOLE] * 3 + [later],
        )(ends, got, first_step, y_f)
        arrived = [swap(send, "seq", 4 * (pairs - 1 - k)) for k, send in enumerate(sends)][::-1]
    y_b, readout_b = local(1, sends[0] if pairs > 1 else got)

    operands = (
        powers, strides, got, leads, starts, y_f, y_b, readout_f, readout_b, z, out_w, *arrived
    )
    half_width = (rows, width // 2)
    gated = (STREAMS, rows, inner)
    both = call(
        functools.partial(finish_kernel, False),
        "finish",
        [shaped(half_width, bf16)] * 2,
        [WHOLE] * len(operands),
        [pltpu.VMEM(gated, bf16)],
    )(*operands)
    first_far, second_far = [swap(send, "seq", 1) for send in both]
    first, gated_own = call(
        functools.partial(finish_kernel, True),
        "finish",
        [shaped(half_width), shaped(gated, bf16)],
        [WHOLE] * len(operands),
    )(*operands)
    first = first + first_far.astype(f32)
    sent = first.astype(bf16)
    if ch_count == 2:
        came = swap(sent, "ch", 1)
    second = call(rest_kernel, "rest", shaped(half_width), [WHOLE] * 2 + [later])(
        gated_own, out_w, sent
    )
    second = second + second_far.astype(f32)
    if ch_count == 2:
        return (second + came.astype(f32)).astype(bf16)
    total = jnp.concatenate([first, second], axis=1)
    return lax.psum_scatter(total.astype(bf16), "ch", scatter_dimension=1, tiled=True)


def solution(mesh):
    placed = (
        P("seq", "ch"),
        P(),
        P(),
        P(),
        P(),
        P(None, None, "ch"),
        P(None, "ch"),
        P("ch"),
        P(None, "ch"),
        P(None, "ch"),
        P("ch"),
        P("ch", None),
    )
    return jax.shard_map(
        body, mesh=mesh, in_specs=placed, out_specs=P("seq", "ch"), check_vma=False
    )
```
